32 devices in a mesh: groups: 2 (over x), sub: 16 (over z, y, core).
Axes of the slice: x: 2, y: 2, z: 4, core: 2. Of those that a mesh axis runs over, the one named last changes fastest.
Arguments:
- heat_source: float32 [8192, 512], P(('groups', 'sub')), parts along dimension 0, may hold values from -6 to 6
- start_temp: float32 [8192, 512], P(('groups', 'sub')), parts along dimension 0, may hold values from -6 to 6
- conduct_shift: float32 [8192, 512], P(('groups', 'sub')), parts along dimension 0, may hold values from 0.02 to 0.5
- slave_face: int32 [32768], P(('groups', 'sub')), parts along dimension 0, may hold values from 0 to 8191, as said below
- master_face: int32 [32768], P(('groups', 'sub')), parts along dimension 0, may hold values from 0 to 8191, as said below
- d_weight: float32 [32768], P(('groups', 'sub')), parts along dimension 0, may hold values from 0.5 to 1.5
- m_weight: float32 [32768], P(('groups', 'sub')), parts along dimension 0, may hold values from 0.3 to 1.2
- gap_cond: float32 [32768], P(('groups', 'sub')), parts along dimension 0, may hold values from 0.5 to 4
- active: int32 [32768], P(('groups', 'sub')), parts along dimension 0, may hold values 0 or 1
Outputs:
- temperature: float32 [8192, 512], P(('groups', 'sub')), parts along dimension 0
- final_residual: float32 [8192, 512], P(('groups', 'sub')), parts along dimension 0
The draws below stay inside these ranges and needn't reach their ends.
There are 2 independent parts, one for each index of `groups`. The reference program is written for one: setup_inputs(seed, part) draws one part's arguments, and reference() takes and returns one part's arrays. A program takes and returns all parts, laid end to end along the dimension named above; each array names one. Nothing has to cross between parts.
Inputs may be any that keep to these rules, and one draw needn't show every extreme that they name: `slave_face`: the face node k * 512 + c belongs to subdomain k. The 1024 pairs listed on one subdomain name slave nodes of exactly 8 subdomains, 128 pairs on each. `master_face`: the 1024 pairs listed on one subdomain name master nodes of exactly 8 subdomains, 128 pairs on each.
All inputs are finite; a program needn't handle non-finite values. No bound on the sum of `active` on one device may be relied on, other than what follows from the above.
Results may differ from the reference program's by a relative error of at most 0.00027.
Values sent between devices are 32-bit elements; how exact they have to be, the bound alone decides.
A program may use at most 64 MiB of HBM per device.

```python
import math
import jax
import jax.numpy as jnp

CX = 256
CY = 512
PAIR_DEV = 1024
OWNER_PAIRS = 128
NEWTON = 2
CG_ITERS = 2
NX = 4096
FACES = 8192
PAIRS = 16384
N_SUB = 16


def faces_from(key):

    def one_block(index):
        block_key = jax.random.fold_in(key, index)
        first, second, third = jax.random.split(block_key, 3)
        owners = jax.random.permutation(first, N_SUB)[:PAIR_DEV // OWNER_PAIRS]
        rows = jnp.repeat(owners, OWNER_PAIRS)
        rows = jax.random.permutation(second, rows)
        offsets = jax.random.randint(third, (PAIR_DEV,), 0, CY)
        return rows * CY + offsets
    return jax.vmap(one_block)(jnp.arange(N_SUB)).reshape(-1).astype(jnp.int32)


def draw_slave_face(key, part):
    key = jax.random.fold_in(key, 11)
    return faces_from(key)


def draw_master_face(key, part):
    key = jax.random.fold_in(key, 23)
    return faces_from(key)


def touch_ends(entries, stream_key, smallest, top_value):
    place = [jax.random.randint(jax.random.fold_in(stream_key, axis), (), 0, length) for axis, length in enumerate(entries.shape)]
    widest = entries.shape.index(max(entries.shape))
    neighbour = place[:widest] + [(place[widest] + 1) % entries.shape[widest]] + place[widest + 1:]
    return entries.at[tuple(place)].set(smallest).at[tuple(neighbour)].set(top_value)


def block_scale(own_key, extent, pieces, low, largest):
    loudness, own = 1.0, jax.random.fold_in(own_key, 6)
    for dim, shards_of in pieces:
        steps = jnp.exp(jax.random.uniform(jax.random.fold_in(own, dim), (shards_of,), jnp.float32, low / len(pieces), largest / len(pieces)))
        loudness = loudness * jnp.repeat(steps, extent[dim] // shards_of).reshape([-1 if axis == dim else 1 for axis in range(len(extent))])
    return loudness


def scatter_about(own_key, shape, spread, bound, cuts=(), dtype=jnp.bfloat16):
    entries = spread * jax.random.normal(own_key, shape, jnp.float32)
    if cuts:
        entries = entries * block_scale(own_key, shape, cuts, -0.22, 0.18)
    return jnp.clip(entries, -bound, bound).astype(dtype)


def setup_inputs(seed: int = 0, part: int = 0) -> dict:
    seeds = jax.random.split(jax.random.key(seed), 10)
    part_keys = jax.random.split(jax.random.fold_in(seeds[9], part), 10)
    return {
        "heat_source": scatter_about(part_keys[0], (NX, CY), 1.0, 6.0, ((0, 16),), jnp.float32),
        "start_temp": scatter_about(part_keys[1], (NX, CY), 1.0, 6.0, ((0, 16),), jnp.float32),
        "conduct_shift": jnp.clip(jnp.exp(math.log(0.5) - 3.218876 * jax.random.uniform(part_keys[2], (NX, CY), jnp.float32) ** block_scale(part_keys[2], (NX, CY), ((0, 16),), -0.2, 0.2)), 0.02, 0.5),
        "slave_face": draw_slave_face(jax.random.fold_in(jax.random.fold_in(seeds[9], part), 71), part),
        "master_face": draw_master_face(jax.random.fold_in(jax.random.fold_in(seeds[9], part), 71), part),
        "d_weight": jnp.clip(0.5 + 1.0 * jax.random.uniform(part_keys[5], (PAIRS,), jnp.float32) ** block_scale(part_keys[5], (PAIRS,), ((0, 16),), -0.2, 0.2), 0.5, 1.5),
        "m_weight": jnp.clip(0.3 + 0.90000004 * jax.random.uniform(part_keys[6], (PAIRS,), jnp.float32) ** block_scale(part_keys[6], (PAIRS,), ((0, 16),), -0.2, 0.2), 0.3, 1.2),
        "gap_cond": jnp.clip(jnp.exp(math.log(4.0) - 2.0794415 * jax.random.uniform(part_keys[7], (PAIRS,), jnp.float32) ** block_scale(part_keys[7], (PAIRS,), ((0, 16),), -0.2, 0.2)), 0.5, 4.0),
        "active": touch_ends((jax.random.randint(part_keys[8], (PAIRS,), 0, 4) < 3).astype(jnp.int32), jax.random.fold_in(part_keys[8], 1), 0, 1),
    }


def stencil(field, shift):
    padded = jnp.pad(field, ((1, 1), (1, 1)))
    beside = padded[2:, 1:-1] + padded[:-2, 1:-1] + padded[1:-1, 2:] + padded[1:-1, :-2]
    return (4.0 + shift) * field - beside


def spread_back(values, slave_face, master_face, d_weight, m_weight, count):
    total = jnp.zeros((count,), jnp.float32)
    total = total.at[slave_face].add(d_weight * values)
    return total.at[master_face].add(-m_weight * values)


def reference(heat_source, start_temp, conduct_shift, slave_face, master_face, d_weight, m_weight, gap_cond, active):
    live = active.astype(jnp.float32) * gap_cond

    def face_row(field):
        return field[::CX].reshape(-1)

    def lifted(field, values):
        return field.at[::CX].add(values.reshape(N_SUB, CY))

    def gap_of(field):
        faces = face_row(field)
        return d_weight * faces[slave_face] - m_weight * faces[master_face]

    def nonlinear(temp):
        gap = gap_of(temp)
        flux = live * (2.0 * gap - jnp.arctan(gap))
        slope = live * (2.0 - 1.0 / (1.0 + gap * gap))
        values = spread_back(flux, slave_face, master_face, d_weight, m_weight, FACES)
        return lifted(stencil(temp, conduct_shift), values) - heat_source, slope

    def jacobian(field, slope):
        values = spread_back(slope * gap_of(field), slave_face, master_face, d_weight, m_weight, FACES)
        return lifted(stencil(field, conduct_shift), values)

    temp = start_temp
    for newton in range(NEWTON):
        resid, slope = nonlinear(temp)
        resvec = -resid
        update = jnp.zeros_like(temp)
        direction = resvec
        norm_now = jnp.sum(resvec * resvec)
        for step in range(CG_ITERS):
            image = jacobian(direction, slope)
            alpha = norm_now / jnp.sum(direction * image)
            update = update + alpha * direction
            resvec = resvec - alpha * image
            norm_next = jnp.sum(resvec * resvec)
            direction = resvec + (norm_next / norm_now) * direction
            norm_now = norm_next
        temp = temp + update
    final_residual, unused = nonlinear(temp)
    return temp, final_residual
```

```python
import functools

import jax
import jax.numpy as jnp
from jax import lax
from jax.experimental import pallas as pl
from jax.experimental.pallas import tpu as pltpu
from jax.sharding import PartitionSpec as P

NEWTON = 2
GATHERS = 1 + 2 * NEWTON
SPREADS = 2 * NEWTON + 1
PARTS = 3
MESH = pl.DeviceIdType.MESH


def arctan(x):
    size = jnp.abs(x)
    large = size > 2.414213562373095
    middle = size > 0.4142135623730950
    top = jnp.where(large, -1.0, jnp.where(middle, size - 1.0, size))
    bottom = jnp.where(large, size, jnp.where(middle, size + 1.0, 1.0))
    base = jnp.where(large, 1.5707963267948966, jnp.where(middle, 0.7853981633974483, 0.0))
    y = top / bottom
    z = y * y
    poly = ((8.05374449538e-2 * z - 1.38776856032e-1) * z + 1.99777106478e-1) * z - 3.33329491539e-1
    result = base + (poly * z * y + y)
    return jnp.where(x < 0.0, -result, result)


def split(x):
    parts = []
    for _ in range(PARTS):
        part = x.astype(jnp.bfloat16)
        parts.append(part)
        x = x - part.astype(jnp.float32)
    return jnp.concatenate(parts, axis=0)


def joined(x):
    rows = x.shape[0] // PARTS
    total = x[:rows]
    for k in range(1, PARTS):
        total = total + x[k * rows:(k + 1) * rows]
    return total


def lanes(row):
    return jnp.concatenate(
        [row[:, k * 128:(k + 1) * 128] for k in range(row.shape[1] // 128)], axis=0
    )


def flat(block):
    return jnp.concatenate([block[k:k + 1] for k in range(block.shape[0])], axis=1)


def partial_sum(x):
    x = jnp.sum(x, axis=0, keepdims=True)
    return jnp.sum(lanes(x), axis=0, keepdims=True)


def whole_sum(x):
    return jnp.sum(x, axis=1, keepdims=True)


def operator(field, shift):
    rows, width = field.shape
    row = lax.broadcasted_iota(jnp.int32, field.shape, 0)
    col = lax.broadcasted_iota(jnp.int32, field.shape, 1)
    up = jnp.where(row == 0, 0.0, pltpu.roll(field, 1, 0))
    down = jnp.where(row == rows - 1, 0.0, pltpu.roll(field, rows - 1, 0))
    left = jnp.where(col == 0, 0.0, pltpu.roll(field, 1, 1))
    right = jnp.where(col == width - 1, 0.0, pltpu.roll(field, width - 1, 1))
    return (4.0 + shift) * field - (up + down + left + right)


def kernel(
    n, heat_ref, start_ref, shift_ref, slave_ref, master_ref, d_ref, m_ref, cond_ref, active_ref,
    temp_ref, final_ref,
    hot, select, faces, kt, r0, kr0, r1, kr1,
    gbuf, hsend_buf, hrecv_buf, csend_buf, crecv_buf, fbuf,
    gsend, grecv, hsend, hrecv, csend, crecv, fsend, frecv,
):
    rows, width = heat_ref.shape
    pairs = slave_ref.shape[1]
    q = width // 128
    me = lax.axis_index("sub")
    group = lax.axis_index("groups")

    def device(j):
        return (group, lax.rem(me + j, n))

    barrier = pltpu.get_barrier_semaphore()

    def greet(j, carry):
        pl.semaphore_signal(barrier, inc=1, device_id=device(j), device_id_type=MESH)
        return carry

    lax.fori_loop(1, n, greet, 0)

    def tables():
        node = lax.broadcasted_iota(jnp.int32, (128, pairs), 0)
        block = lax.broadcasted_iota(jnp.int32, (n * q, pairs), 0)
        for k, (ref, weight) in enumerate(((slave_ref, d_ref[...]), (master_ref, -m_ref[...]))):
            face = ref[...]
            low = jnp.bitwise_and(face, 127)
            high = jnp.right_shift(face, 7)
            here = pl.ds(k * pairs, pairs)
            hot[:, here] = jnp.where(node == low, 1.0, 0.0).astype(jnp.bfloat16)
            select[:, here] = jnp.where(block == high, weight, 0.0)

    tables()
    pl.semaphore_wait(barrier, n - 1)

    def send_all(source, target, send_sem, recv_sem):
        def send(j, carry):
            to = lax.rem(me + j, n)
            pltpu.make_async_remote_copy(
                src_ref=source(to), dst_ref=target, send_sem=send_sem, recv_sem=recv_sem,
                device_id=(group, to), device_id_type=MESH,
            ).start()
            return carry

        lax.fori_loop(1, n, send, 0)

    def wait_all(buffer, sem):
        part = buffer.at[pl.ds(0, n - 1)]
        pltpu.make_async_copy(part, part, sem).wait()

    def gather_start(k, field, partial):
        gbuf[k, me, 0:q] = lanes(field[0:1])
        if partial is not None:
            gbuf[k, me, q:q + 1] = partial
        hsend_buf[k, 0:q] = lanes(field[rows - 1:rows])
        send_all(lambda to: gbuf.at[k, me], gbuf.at[k, me], gsend.at[k], grecv.at[k])
        halo_copy(k).start()

    def halo_copy(k):
        return pltpu.make_async_remote_copy(
            src_ref=hsend_buf.at[k], dst_ref=hrecv_buf.at[k], send_sem=hsend.at[k],
            recv_sem=hrecv.at[k], device_id=device(1), device_id_type=MESH,
        )

    def gather_end(k, partial):
        wait_all(gbuf.at[k], grecv.at[k])
        halo_copy(k).wait_recv()
        for j in range(n):
            faces[j * q:(j + 1) * q] = gbuf[k, j, 0:q]
        values = joined(
            jnp.dot(split(faces[...]), hot[...], preferred_element_type=jnp.float32)
        )
        ends = jnp.sum(values * select[...], axis=0, keepdims=True)
        gap = ends[:, :pairs] + ends[:, pairs:]
        above = jnp.where(me == 0, 0.0, flat(hrecv_buf[k, 0:q]))
        below = gbuf[k, lax.rem(me + 1, n), 0:q]
        below = jnp.where(me == n - 1, 0.0, flat(below))
        if partial:
            return gap, above, below, whole_sum(jnp.sum(gbuf[k, :, q:q + 1], axis=0))
        return gap, above, below

    def spread_start(k, flux, partial):
        weighted = select[...] * jnp.concatenate([flux, flux], axis=1)
        total = joined(
            lax.dot_general(
                split(weighted), hot[...], (((1,), (1,)), ((), ())),
                preferred_element_type=jnp.float32,
            )
        )
        for j in range(n):
            csend_buf[k, j, 0:q] = total[j * q:(j + 1) * q]
            if partial is not None:
                csend_buf[k, j, q:q + 1] = partial
        send_all(lambda to: csend_buf.at[k, to], crecv_buf.at[k, me], csend.at[k], crecv.at[k])
        crecv_buf[k, me, 0:q + 1] = csend_buf[k, me, 0:q + 1]

    def spread_end(k, partial):
        wait_all(crecv_buf.at[k], crecv.at[k])
        lift = flat(jnp.sum(crecv_buf[k, :, 0:q], axis=0))
        if partial:
            return lift, whole_sum(jnp.sum(crecv_buf[k, :, q:q + 1], axis=0))
        return lift

    def with_halo(ref, above, below):
        ref[0:1] = ref[0:1] - above
        ref[rows - 1:rows] = ref[rows - 1:rows] - below

    shift = shift_ref[...]
    live = active_ref[...].astype(jnp.float32) * cond_ref[...]

    gather_start(0, start_ref, None)
    kt[...] = operator(start_ref[...], shift) - heat_ref[...]
    gap_t, above, below = gather_end(0, False)
    with_halo(kt, above, below)
    for newton in range(NEWTON):
        first, second = 1 + 2 * newton, 2 + 2 * newton
        flux = live * (2.0 * gap_t - arctan(gap_t))
        spread_start(2 * newton, flux, None)
        slope = live * (2.0 - 1.0 / (1.0 + gap_t * gap_t))
        r0[...] = -kt[...]
        lift = spread_end(2 * newton, False)
        r0[0:1] = r0[0:1] - lift

        gather_start(first, r0, partial_sum(r0[...] * r0[...]))
        kr0[...] = operator(r0[...], shift)
        gap_0, above, below, rr = gather_end(first, True)
        with_halo(kr0, above, below)

        push = slope * gap_0
        spread_start(
            2 * newton + 1, push, partial_sum(r0[...] * kr0[...]) + partial_sum(push * gap_0)
        )
        lift, curve = spread_end(2 * newton + 1, True)
        alpha = rr / curve
        r1[...] = r0[...] - alpha * kr0[...]
        r1[0:1] = r1[0:1] - alpha * lift

        gather_start(second, r1, partial_sum(r1[...] * r1[...]))
        kr1[...] = operator(r1[...], shift)
        gap_1, above, below, rr_next = gather_end(second, True)
        with_halo(kr1, above, below)
        beta = rr_next / rr
        r1[...] = r1[...] + beta * r0[...]
        kr1[...] = kr1[...] + beta * kr0[...]
        gap_1 = gap_1 + beta * gap_0
        fbuf[newton, me] = partial_sum(r1[...] * kr1[...]) + partial_sum(slope * gap_1 * gap_1)
        send_all(
            lambda to: fbuf.at[newton, me], fbuf.at[newton, me], fsend.at[newton], frecv.at[newton]
        )
        temp = start_ref if newton == 0 else temp_ref
        temp_ref[...] = temp[...] + alpha * r0[...]
        kt[...] = kt[...] + alpha * kr0[...]
        wait_all(fbuf.at[newton], frecv.at[newton])
        alpha_next = rr_next / whole_sum(jnp.sum(fbuf[newton], axis=0))
        temp_ref[...] = temp_ref[...] + alpha_next * r1[...]
        kt[...] = kt[...] + alpha_next * kr1[...]
        gap_t = gap_t + alpha * gap_0 + alpha_next * gap_1

    flux = live * (2.0 * gap_t - arctan(gap_t))
    spread_start(2 * NEWTON, flux, None)
    final_ref[...] = kt[...]
    lift = spread_end(2 * NEWTON, False)
    final_ref[0:1] = final_ref[0:1] + lift

    for k in range(GATHERS):
        wait_all(gbuf.at[k], gsend.at[k])
        halo_copy(k).wait_send()
    for k in range(SPREADS):
        wait_all(csend_buf.at[k], csend.at[k])
    for k in range(NEWTON):
        wait_all(fbuf.at[k], fsend.at[k])


def on_device(heat, start, shift, slave, master, d_weight, m_weight, gap_cond, active):
    n = lax.axis_size("sub")
    rows, width = heat.shape
    pairs = slave.shape[0]
    q = width // 128
    tall = (q + 1 + 7) // 8 * 8
    field = pltpu.VMEM((rows, width), jnp.float32)
    sems = lambda count: pltpu.SemaphoreType.DMA((count,))
    vmem = pl.BlockSpec(memory_space=pltpu.VMEM)
    across = lambda x: x.reshape(1, pairs)
    return pl.pallas_call(
        functools.partial(kernel, n),
        out_shape=(jax.ShapeDtypeStruct((rows, width), jnp.float32),) * 2,
        in_specs=[vmem] * 9,
        out_specs=(vmem, vmem),
        scratch_shapes=[
            pltpu.VMEM((128, 2 * pairs), jnp.bfloat16),
            pltpu.VMEM((n * q, 2 * pairs), jnp.float32),
            pltpu.VMEM((n * q, 128), jnp.float32),
            field, field, field, field, field,
            pltpu.VMEM((GATHERS, n, tall, 128), jnp.float32),
            pltpu.VMEM((GATHERS, tall, 128), jnp.float32),
            pltpu.VMEM((GATHERS, tall, 128), jnp.float32),
            pltpu.VMEM((SPREADS, n, tall, 128), jnp.float32),
            pltpu.VMEM((SPREADS, n, tall, 128), jnp.float32),
            pltpu.VMEM((NEWTON, n, 1, 128), jnp.float32),
            sems(GATHERS), sems(GATHERS), sems(GATHERS), sems(GATHERS),
            sems(SPREADS), sems(SPREADS), sems(NEWTON), sems(NEWTON),
        ],
        compiler_params=pltpu.CompilerParams(
            collective_id=0, has_side_effects=True, vmem_limit_bytes=48 * 2**20
        ),
    )(
        heat, start, shift, across(slave), across(master), across(d_weight), across(m_weight),
        across(gap_cond), across(active),
    )


def solution(mesh):
    field = P(("groups", "sub"), None)
    pair = P(("groups", "sub"))
    return jax.shard_map(
        on_device, mesh=mesh, in_specs=(field,) * 3 + (pair,) * 6, out_specs=(field, field),
        check_vma=False,
    )
```

```python
import functools

import jax
import jax.numpy as jnp
from jax import lax
from jax.experimental import pallas as pl
from jax.experimental.pallas import tpu as pltpu
from jax.sharding import PartitionSpec as P

NEWTON = 2
GATHERS = 1 + 2 * NEWTON
PARTS = 3
MESH = pl.DeviceIdType.MESH


def arctan(x):
    size = jnp.abs(x)
    large = size > 2.414213562373095
    middle = size > 0.4142135623730950
    top = jnp.where(large, -1.0, jnp.where(middle, size - 1.0, size))
    bottom = jnp.where(large, size, jnp.where(middle, size + 1.0, 1.0))
    base = jnp.where(large, 1.5707963267948966, jnp.where(middle, 0.7853981633974483, 0.0))
    y = top / bottom
    z = y * y
    poly = ((8.05374449538e-2 * z - 1.38776856032e-1) * z + 1.99777106478e-1) * z - 3.33329491539e-1
    result = base + (poly * z * y + y)
    return jnp.where(x < 0.0, -result, result)


def split(x, count):
    parts = []
    for _ in range(count):
        part = x.astype(jnp.bfloat16).astype(jnp.float32)
        parts.append(part)
        x = x - part
    return jnp.concatenate(parts, axis=0).astype(jnp.bfloat16)


def joined(x, count):
    rows = x.shape[0] // count
    total = x[:rows]
    for k in range(1, count):
        total = total + x[k * rows:(k + 1) * rows]
    return total


def lanes(row):
    return jnp.concatenate(
        [row[:, k * 128:(k + 1) * 128] for k in range(row.shape[1] // 128)], axis=0
    )


def flat(block):
    return jnp.concatenate([block[k:k + 1] for k in range(block.shape[0])], axis=1)


def partial_sum(x):
    x = jnp.sum(x, axis=0, keepdims=True)
    return jnp.sum(lanes(x), axis=0, keepdims=True)


def whole_sum(x):
    return jnp.sum(x, axis=1, keepdims=True)


def operator(field, shift):
    rows, width = field.shape
    row = lax.broadcasted_iota(jnp.int32, field.shape, 0)
    col = lax.broadcasted_iota(jnp.int32, field.shape, 1)
    up = jnp.where(row == 0, 0.0, pltpu.roll(field, 1, 0))
    down = jnp.where(row == rows - 1, 0.0, pltpu.roll(field, rows - 1, 0))
    left = jnp.where(col == 0, 0.0, pltpu.roll(field, 1, 1))
    right = jnp.where(col == width - 1, 0.0, pltpu.roll(field, width - 1, 1))
    return (4.0 + shift) * field - (up + down + left + right)


def kernel(
    n, heat_ref, start_ref, shift_ref, slave_ref, master_ref, d_ref, m_ref, cond_ref, active_ref,
    temp_ref, final_ref,
    hot_own, hot_other, pick_own, pick_other, faces, kt, r0, kr0, w0, kw0, r1,
    gbuf, hsend_buf, hrecv_buf, rsend_buf, rrecv_buf, fbuf,
    gsend, grecv, hsend, hrecv, rsend, rrecv, fsend, frecv,
):
    rows, width = heat_ref.shape
    pairs = slave_ref.shape[1]
    q = width // 128
    slots = rsend_buf.shape[2]
    listed = hot_own.shape[1]
    me = lax.axis_index("sub")
    group = lax.axis_index("groups")

    def device(j):
        return (group, lax.rem(me + j, n))

    barrier = pltpu.get_barrier_semaphore()

    def greet(j, carry):
        pl.semaphore_signal(barrier, inc=1, device_id=device(j), device_id_type=MESH)
        return carry

    lax.fori_loop(1, n, greet, 0)

    def send_all(source, target, send_sem, recv_sem):
        def send(j, carry):
            to = lax.rem(me + j, n)
            pltpu.make_async_remote_copy(
                src_ref=source(to), dst_ref=target, send_sem=send_sem, recv_sem=recv_sem,
                device_id=(group, to), device_id_type=MESH,
            ).start()
            return carry

        lax.fori_loop(1, n, send, 0)

    def wait_all(buffer, sem):
        part = buffer.at[pl.ds(0, n - 1)]
        pltpu.make_async_copy(part, part, sem).wait()

    def records():
        slave, master = slave_ref[...], master_ref[...]
        d, m = d_ref[...], -m_ref[...]
        live = active_ref[...].astype(jnp.float32) * cond_ref[...]
        log = width.bit_length() - 1
        block = lax.broadcasted_iota(jnp.int32, (n, pairs), 0)
        upto = lax.broadcasted_iota(jnp.int32, (128, 128), 0) <= lax.broadcasted_iota(
            jnp.int32, (128, 128), 1
        )
        upto = jnp.where(upto, 1.0, 0.0).astype(jnp.bfloat16)
        slot = lax.broadcasted_iota(jnp.int32, (slots, pairs), 0)
        owners, fields, places = [], [], []
        for own, other, mine, theirs in ((slave, master, d, m), (master, slave, m, d)):
            owner = jnp.right_shift(own, log)
            named = jnp.where(block == owner, 1.0, 0.0)
            chunks = [named[:, k:k + 128] for k in range(0, pairs, 128)]
            counts = jnp.dot(
                jnp.concatenate(chunks, axis=0).astype(jnp.bfloat16), upto,
                preferred_element_type=jnp.float32,
            )
            before = jnp.zeros((n, 1), jnp.float32)
            ranks = []
            for k, chunk in enumerate(chunks):
                count = counts[k * n:(k + 1) * n] + before
                before = count[:, 127:128]
                ranks.append(jnp.sum(count * chunk, axis=0, keepdims=True) - 1.0)
            rank = jnp.concatenate(ranks, axis=1).astype(jnp.int32)
            places.append(jnp.where(slot == rank, 1.0, 0.0).astype(jnp.bfloat16))
            code = other * width + jnp.bitwise_and(own, width - 1)
            fields += [code.astype(jnp.float32), mine, theirs, live]
            owners += [owner] * 4
        fields = jnp.concatenate(fields, axis=0)[None]
        owners = jnp.concatenate(owners, axis=0)[None]
        block = lax.broadcasted_iota(jnp.int32, (n, 8, pairs), 0)
        spread = jnp.where(block == owners, fields, 0.0).reshape(8 * n, pairs)
        placed = joined(
            lax.dot_general(
                split(spread, 3), jnp.concatenate(places, axis=0), (((1,), (1,)), ((), ())),
                preferred_element_type=jnp.float32,
            ),
            3,
        )
        row = jnp.bitwise_and(lax.broadcasted_iota(jnp.int32, (8 * n, slots), 0), 7)
        placed = jnp.where(row < 4, placed[:, :slots], placed[:, slots:])
        rsend_buf[...] = placed.reshape(n, 8, slots)

    def field_of(k):
        return jnp.concatenate(
            [rrecv_buf[j, k + role:k + role + 1] for role in (0, 4) for j in range(n)], axis=1
        )

    def tables():
        code = field_of(0).astype(jnp.int32)
        own = jnp.bitwise_and(code, width - 1)
        other = jnp.right_shift(code, width.bit_length() - 1)
        node = lax.broadcasted_iota(jnp.int32, (128, listed), 0)
        for hot, face, pick, weight in (
            (hot_own, own, pick_own, field_of(1)), (hot_other, other, pick_other, field_of(2))
        ):
            low, high = jnp.bitwise_and(face, 127), jnp.right_shift(face, 7)
            hot[...] = jnp.where(node == low, 1.0, 0.0).astype(jnp.bfloat16)
            block = lax.broadcasted_iota(jnp.int32, pick.shape, 0)
            pick[...] = jnp.where(block == high, weight, 0.0)
        return field_of(3)

    def ends(rows_of, hot, pick):
        parts = split(rows_of, PARTS)
        pieces = []
        step = min(listed, 2048)
        for k in range(0, listed, step):
            here = pl.ds(k, step)
            values = joined(
                jnp.dot(parts, hot[:, here], preferred_element_type=jnp.float32), PARTS
            )
            pieces.append(jnp.sum(values * pick[:, here], axis=0, keepdims=True))
        return jnp.concatenate(pieces, axis=1)

    def lift_of(flux):
        total = joined(
            lax.dot_general(
                split(pick_own[...] * flux, PARTS), hot_own[...], (((1,), (1,)), ((), ())),
                preferred_element_type=jnp.float32,
            ),
            PARTS,
        )
        return flat(total[0:q])

    def gather_start(k, field, partial):
        gbuf[k, me, 0:q] = lanes(field[0:1])
        if partial is not None:
            gbuf[k, me, q:q + 1] = partial
        hsend_buf[k, 0:q] = lanes(field[rows - 1:rows])
        send_all(lambda to: gbuf.at[k, me], gbuf.at[k, me], gsend.at[k], grecv.at[k])
        halo_copy(k).start()

    def halo_copy(k):
        return pltpu.make_async_remote_copy(
            src_ref=hsend_buf.at[k], dst_ref=hrecv_buf.at[k], send_sem=hsend.at[k],
            recv_sem=hrecv.at[k], device_id=device(1), device_id_type=MESH,
        )

    def own_ends(field):
        own = jnp.concatenate(
            [lanes(field[0:1]), jnp.zeros((pick_own.shape[0] - q, 128), jnp.float32)], axis=0
        )
        return ends(own, hot_own, pick_own)

    def gather_end(k):
        wait_all(gbuf.at[k], grecv.at[k])
        halo_copy(k).wait_recv()
        for j in range(n):
            faces[j * q:(j + 1) * q] = gbuf[k, j, 0:q]

    def halos(k, ref):
        above = jnp.where(me == 0, 0.0, flat(hrecv_buf[k, 0:q]))
        below = gbuf[k, lax.rem(me + 1, n), 0:q]
        below = jnp.where(me == n - 1, 0.0, flat(below))
        ref[0:1] = ref[0:1] - above
        ref[rows - 1:rows] = ref[rows - 1:rows] - below

    def total_of(k):
        return whole_sum(jnp.sum(gbuf[k, :, q:q + 1], axis=0))

    shift = shift_ref[...]
    records()
    pl.semaphore_wait(barrier, n - 1)
    send_all(lambda to: rsend_buf.at[to], rrecv_buf.at[me], rsend.at[0], rrecv.at[0])
    gather_start(0, start_ref, None)
    rrecv_buf[me] = rsend_buf[me]
    kt[...] = operator(start_ref[...], shift) - heat_ref[...]
    wait_all(rrecv_buf, rrecv.at[0])
    live = tables()
    gather_end(0)
    halos(0, kt)
    gap_t = own_ends(start_ref) + ends(faces[...], hot_other, pick_other)

    for newton in range(NEWTON):
        first, second = 1 + 2 * newton, 2 + 2 * newton
        lift = lift_of(live * (2.0 * gap_t - arctan(gap_t)))
        r0[...] = -kt[...]
        r0[0:1] = r0[0:1] - lift

        gather_start(first, r0, partial_sum(r0[...] * r0[...]))
        kr0[...] = operator(r0[...], shift)
        slope = live * (2.0 - 1.0 / (1.0 + gap_t * gap_t))
        gap_0 = own_ends(r0)
        gather_end(first)
        halos(first, kr0)
        gap_0 = gap_0 + ends(faces[...], hot_other, pick_other)
        lift = lift_of(slope * gap_0)
        w0[...] = kr0[...]
        w0[0:1] = w0[0:1] + lift

        gather_start(second, w0, partial_sum(r0[...] * w0[...]))
        rr = total_of(first)
        kw0[...] = operator(w0[...], shift)
        gap_w = own_ends(w0)
        gather_end(second)
        halos(second, kw0)
        curve = total_of(second)
        alpha = rr / curve
        gap_w = gap_w + ends(faces[...], hot_other, pick_other)
        lift = lift_of(slope * gap_w)
        r1[...] = r0[...] - alpha * w0[...]
        residual = r1[...]
        fbuf[newton, me, 0:1] = partial_sum(residual * residual)
        fbuf[newton, me, 1:2] = partial_sum(residual * w0[...])
        fbuf[newton, me, 2:3] = partial_sum(
            residual * (w0[...] - alpha * kw0[...])
        ) - alpha * partial_sum(residual[0:1] * lift)
        send_all(
            lambda to: fbuf.at[newton, me], fbuf.at[newton, me], fsend.at[newton], frecv.at[newton]
        )
        temp = start_ref if newton == 0 else temp_ref
        temp_ref[...] = temp[...] + alpha * r0[...]
        kt[...] = kt[...] + alpha * kr0[...]
        gap_t = gap_t + alpha * gap_0
        gap_1 = gap_0 - alpha * gap_w
        wait_all(fbuf.at[newton], frecv.at[newton])
        sums = whole_sum(jnp.sum(fbuf[newton], axis=0))
        rr_next, cross, inner = sums[0:1], sums[1:2], sums[2:3]
        beta = rr_next / rr
        alpha_next = rr_next / (inner + 2.0 * beta * cross + beta * beta * curve)
        gap_t = gap_t + alpha_next * (gap_1 + beta * gap_0)
        kt[...] = kt[...] + alpha_next * (kr0[...] - alpha * kw0[...] + beta * kr0[...])
        temp_ref[...] = temp_ref[...] + alpha_next * (r1[...] + beta * r0[...])

    lift = lift_of(live * (2.0 * gap_t - arctan(gap_t)))
    final_ref[...] = kt[...]
    final_ref[0:1] = final_ref[0:1] + lift

    for k in range(GATHERS):
        wait_all(gbuf.at[k], gsend.at[k])
        halo_copy(k).wait_send()
    wait_all(rsend_buf, rsend.at[0])
    for k in range(NEWTON):
        wait_all(fbuf.at[k], fsend.at[k])


def on_device(heat, start, shift, slave, master, d_weight, m_weight, gap_cond, active):
    n = lax.axis_size("sub")
    rows, width = heat.shape
    pairs = slave.shape[0]
    q = width // 128
    slots = pairs // 8
    listed = 2 * n * slots
    tall = (q + 1 + 7) // 8 * 8
    own_rows = (q + 7) // 8 * 8
    field = pltpu.VMEM((rows, width), jnp.float32)
    sems = lambda count: pltpu.SemaphoreType.DMA((count,))
    vmem = pl.BlockSpec(memory_space=pltpu.VMEM)
    across = lambda x: x.reshape(1, pairs)
    return pl.pallas_call(
        functools.partial(kernel, n),
        out_shape=(jax.ShapeDtypeStruct((rows, width), jnp.float32),) * 2,
        in_specs=[vmem] * 9,
        out_specs=(vmem, vmem),
        scratch_shapes=[
            pltpu.VMEM((128, listed), jnp.bfloat16),
            pltpu.VMEM((128, listed), jnp.bfloat16),
            pltpu.VMEM((own_rows, listed), jnp.float32),
            pltpu.VMEM((n * q, listed), jnp.float32),
            pltpu.VMEM((n * q, 128), jnp.float32),
            field, field, field, field, field, field,
            pltpu.VMEM((GATHERS, n, tall, 128), jnp.float32),
            pltpu.VMEM((GATHERS, tall, 128), jnp.float32),
            pltpu.VMEM((GATHERS, tall, 128), jnp.float32),
            pltpu.VMEM((n, 8, slots), jnp.float32),
            pltpu.VMEM((n, 8, slots), jnp.float32),
            pltpu.VMEM((NEWTON, n, 8, 128), jnp.float32),
            sems(GATHERS), sems(GATHERS), sems(GATHERS), sems(GATHERS),
            sems(1), sems(1), sems(NEWTON), sems(NEWTON),
        ],
        compiler_params=pltpu.CompilerParams(
            collective_id=0, has_side_effects=True, vmem_limit_bytes=48 * 2**20
        ),
    )(
        heat, start, shift, across(slave), across(master), across(d_weight), across(m_weight),
        across(gap_cond), across(active),
    )


def solution(mesh):
    field = P(("groups", "sub"), None)
    pair = P(("groups", "sub"))
    return jax.shard_map(
        on_device, mesh=mesh, in_specs=(field,) * 3 + (pair,) * 6, out_specs=(field, field),
        check_vma=False,
    )
```

```python
import functools

import jax
import jax.numpy as jnp
from jax import lax
from jax.experimental import pallas as pl
from jax.experimental.pallas import tpu as pltpu
from jax.sharding import PartitionSpec as P

NEWTON = 2
GATHERS = 1 + 2 * NEWTON
PARTS = 2
MESH = pl.DeviceIdType.MESH


def arctan(x):
    size = jnp.abs(x)
    large = size > 2.414213562373095
    middle = size > 0.4142135623730950
    top = jnp.where(large, -1.0, jnp.where(middle, size - 1.0, size))
    bottom = jnp.where(large, size, jnp.where(middle, size + 1.0, 1.0))
    base = jnp.where(large, 1.5707963267948966, jnp.where(middle, 0.7853981633974483, 0.0))
    y = top / bottom
    z = y * y
    poly = ((8.05374449538e-2 * z - 1.38776856032e-1) * z + 1.99777106478e-1) * z - 3.33329491539e-1
    result = base + (poly * z * y + y)
    return jnp.where(x < 0.0, -result, result)


def split(x, count):
    parts = []
    for _ in range(count):
        part = x.astype(jnp.bfloat16).astype(jnp.float32)
        parts.append(part)
        x = x - part
    return jnp.concatenate(parts, axis=0).astype(jnp.bfloat16)


def joined(x, count):
    rows = x.shape[0] // count
    total = x[:rows]
    for k in range(1, count):
        total = total + x[k * rows:(k + 1) * rows]
    return total


def lanes(row):
    return jnp.concatenate(
        [row[:, k * 128:(k + 1) * 128] for k in range(row.shape[1] // 128)], axis=0
    )


def flat(block):
    return jnp.concatenate([block[k:k + 1] for k in range(block.shape[0])], axis=1)


def partial_sum(x):
    x = jnp.sum(x, axis=0, keepdims=True)
    return jnp.sum(lanes(x), axis=0, keepdims=True)


def whole_sum(x):
    return jnp.sum(x, axis=1, keepdims=True)


def operator(field, shift):
    rows, width = field.shape
    row = lax.broadcasted_iota(jnp.int32, field.shape, 0)
    col = lax.broadcasted_iota(jnp.int32, field.shape, 1)
    up = jnp.where(row == 0, 0.0, pltpu.roll(field, 1, 0))
    down = jnp.where(row == rows - 1, 0.0, pltpu.roll(field, rows - 1, 0))
    left = jnp.where(col == 0, 0.0, pltpu.roll(field, 1, 1))
    right = jnp.where(col == width - 1, 0.0, pltpu.roll(field, width - 1, 1))
    return (4.0 + shift) * field - (up + down + left + right)


def kernel(
    n, heat_in, start_in, shift_in, slave_in, master_in, d_in, m_in, cond_in, active_in,
    temp_ref, final_ref,
    heat_ref, start_ref, shift_ref, slave_ref, master_ref, d_ref, m_ref, cond_ref, active_ref,
    hot_own, hot_other, pick_own, pick_other, faces, kt, r0, w0, kw0,
    plain_buf, sums_buf, hsend_buf, hrecv_buf, rsend_buf, rrecv_buf, fbuf,
    loads, gsend, grecv, hsend, hrecv, rsend, rrecv, fsend, frecv,
):
    inputs = [
        pltpu.make_async_copy(source, target, loads.at[k])
        for k, (source, target) in enumerate((
            (slave_in, slave_ref), (master_in, master_ref), (d_in, d_ref), (m_in, m_ref),
            (cond_in, cond_ref), (active_in, active_ref), (start_in, start_ref),
            (shift_in, shift_ref), (heat_in, heat_ref),
        ))
    ]
    for copy in inputs:
        copy.start()
    rows, width = heat_ref.shape
    pairs = slave_ref.shape[1]
    q = width // 128
    slots = rsend_buf.shape[2]
    listed = hot_own.shape[1]
    me = lax.axis_index("sub")
    group = lax.axis_index("groups")

    def device(j):
        return (group, lax.rem(me + j, n))

    barrier = pltpu.get_barrier_semaphore()

    def greet(j, carry):
        pl.semaphore_signal(barrier, inc=1, device_id=device(j), device_id_type=MESH)
        return carry

    lax.fori_loop(1, n, greet, 0)

    def send_all(source, target, send_sem, recv_sem):
        def send(j, carry):
            to = lax.rem(me + j, n)
            pltpu.make_async_remote_copy(
                src_ref=source(to), dst_ref=target, send_sem=send_sem, recv_sem=recv_sem,
                device_id=(group, to), device_id_type=MESH,
            ).start()
            return carry

        lax.fori_loop(1, n, send, 0)

    def wait_all(buffer, sem):
        part = buffer.at[pl.ds(0, n - 1)]
        pltpu.make_async_copy(part, part, sem).wait()

    def records():
        slave, master = slave_ref[...], master_ref[...]
        d, m = d_ref[...], -m_ref[...]
        live = active_ref[...].astype(jnp.float32) * cond_ref[...]
        log = width.bit_length() - 1
        block = lax.broadcasted_iota(jnp.int32, (n, pairs), 0)
        upto = lax.broadcasted_iota(jnp.int32, (128, 128), 0) <= lax.broadcasted_iota(
            jnp.int32, (128, 128), 1
        )
        upto = jnp.where(upto, 1.0, 0.0).astype(jnp.bfloat16)
        slot = lax.broadcasted_iota(jnp.int32, (slots, pairs), 0)
        owners, fields, places = [], [], []
        for own, other, mine, theirs in ((slave, master, d, m), (master, slave, m, d)):
            owner = jnp.right_shift(own, log)
            named = jnp.where(block == owner, 1.0, 0.0)
            chunks = [named[:, k:k + 128] for k in range(0, pairs, 128)]
            counts = jnp.dot(
                jnp.concatenate(chunks, axis=0).astype(jnp.bfloat16), upto,
                preferred_element_type=jnp.float32,
            )
            before = jnp.zeros((n, 1), jnp.float32)
            ranks = []
            for k, chunk in enumerate(chunks):
                count = counts[k * n:(k + 1) * n] + before
                before = count[:, 127:128]
                ranks.append(jnp.sum(count * chunk, axis=0, keepdims=True) - 1.0)
            rank = jnp.concatenate(ranks, axis=1).astype(jnp.int32)
            places.append(jnp.where(slot == rank, 1.0, 0.0).astype(jnp.bfloat16))
            code = other * width + jnp.bitwise_and(own, width - 1)
            fields += [code.astype(jnp.float32), mine, theirs, live]
            owners += [owner] * 4
        fields = jnp.concatenate(fields, axis=0)[None]
        owners = jnp.concatenate(owners, axis=0)[None]
        block = lax.broadcasted_iota(jnp.int32, (n, 8, pairs), 0)
        spread = jnp.where(block == owners, fields, 0.0).reshape(8 * n, pairs)
        placed = joined(
            lax.dot_general(
                split(spread, 3), jnp.concatenate(places, axis=0), (((1,), (1,)), ((), ())),
                preferred_element_type=jnp.float32,
            ),
            3,
        )
        row = jnp.bitwise_and(lax.broadcasted_iota(jnp.int32, (8 * n, slots), 0), 7)
        placed = jnp.where(row < 4, placed[:, :slots], placed[:, slots:])
        rsend_buf[...] = placed.reshape(n, 8, slots)

    def field_of(k):
        return jnp.concatenate(
            [rrecv_buf[j, k + role:k + role + 1] for role in (0, 4) for j in range(n)], axis=1
        )

    def tables():
        code = field_of(0).astype(jnp.int32)
        own = jnp.bitwise_and(code, width - 1)
        other = jnp.right_shift(code, width.bit_length() - 1)
        node = lax.broadcasted_iota(jnp.int32, (128, listed), 0)
        for hot, face, pick, weight in (
            (hot_own, own, pick_own, field_of(1)), (hot_other, other, pick_other, field_of(2))
        ):
            low, high = jnp.bitwise_and(face, 127), jnp.right_shift(face, 7)
            hot[...] = jnp.where(node == low, 1.0, 0.0).astype(jnp.bfloat16)
            block = lax.broadcasted_iota(jnp.int32, pick.shape, 0)
            pick[...] = jnp.where(block == high, weight, 0.0)
        return field_of(3)

    def ends(rows_of, hot, pick):
        parts = split(rows_of, PARTS)
        pieces = []
        step = min(listed, 2048)
        for k in range(0, listed, step):
            here = pl.ds(k, step)
            values = joined(
                jnp.dot(parts, hot[:, here], preferred_element_type=jnp.float32), PARTS
            )
            pieces.append(jnp.sum(values * pick[:, here], axis=0, keepdims=True))
        return jnp.concatenate(pieces, axis=1)

    def lift_of(flux):
        total = joined(
            lax.dot_general(
                split(pick_own[...] * flux, PARTS), hot_own[...], (((1,), (1,)), ((), ())),
                preferred_element_type=jnp.float32,
            ),
            PARTS,
        )
        return flat(total[0:q])

    def slab(k):
        if k > 0 and k % 2 == 0:
            return sums_buf.at[k // 2 - 1]
        return plain_buf.at[(k + 1) // 2]

    def gather_start(k, top, bottom, partials=()):
        buffer = slab(k)
        buffer[me, 0:q] = lanes(top)
        for place, partial in enumerate(partials):
            buffer[me, q + place:q + place + 1] = partial
        hsend_buf[k] = lanes(bottom)
        send_all(lambda to: buffer.at[me], buffer.at[me], gsend.at[k], grecv.at[k])
        halo_copy(k).start()

    def halo_copy(k):
        return pltpu.make_async_remote_copy(
            src_ref=hsend_buf.at[k], dst_ref=hrecv_buf.at[k], send_sem=hsend.at[k],
            recv_sem=hrecv.at[k], device_id=device(1), device_id_type=MESH,
        )

    def own_ends(top):
        own = jnp.concatenate(
            [lanes(top), jnp.zeros((pick_own.shape[0] - q, 128), jnp.float32)], axis=0
        )
        return ends(own, hot_own, pick_own)

    def gather_end(k):
        buffer = slab(k)
        wait_all(buffer, grecv.at[k])
        halo_copy(k).wait_recv()
        for j in range(n):
            faces[j * q:(j + 1) * q] = buffer[j, 0:q]
        above = jnp.where(me == 0, 0.0, flat(hrecv_buf[k]))
        below = jnp.where(me == n - 1, 0.0, flat(buffer[lax.rem(me + 1, n), 0:q]))
        return ends(faces[...], hot_other, pick_other), above, below

    def lane_sum(row):
        return jnp.sum(lanes(row), axis=0, keepdims=True)

    first_row, last_row = pl.ds(0, 1), pl.ds(rows - 1, 1)

    for copy in inputs[:6]:
        copy.wait()
    records()
    inputs[6].wait()
    pl.semaphore_wait(barrier, n - 1)
    send_all(lambda to: rsend_buf.at[to], rrecv_buf.at[me], rsend.at[0], rrecv.at[0])
    gather_start(0, start_ref[first_row], start_ref[last_row])
    rrecv_buf[me] = rsend_buf[me]
    inputs[7].wait()
    inputs[8].wait()
    kt[...] = operator(start_ref[...], shift_ref[...]) - heat_ref[...]
    wait_all(rrecv_buf, rrecv.at[0])
    live = tables()
    gap_t = own_ends(start_ref[first_row])
    gap_other, above, below = gather_end(0)
    gap_t = gap_t + gap_other
    kt[first_row] = kt[first_row] - above
    kt[last_row] = kt[last_row] - below
    top, bottom = -kt[first_row], -kt[last_row]

    for newton in range(NEWTON):
        first, second = 1 + 2 * newton, 2 + 2 * newton
        top = top - lift_of(live * (2.0 * gap_t - arctan(gap_t)))
        gather_start(first, top, bottom)
        if newton > 0:
            kt[...] = kt[...] + (step_0 * w0[...] + step_w * kw0[...])
            kt[first_row] = kt[first_row] - step_0 * lift_0
            temp_ref[...] = temp_ref[...] + (step_0 * r0[...] + step_w * w0[...])
        else:
            temp_ref[...] = start_ref[...]
        r0[...] = -kt[...]
        r0[first_row] = top
        r0[last_row] = bottom
        w0[...] = operator(r0[...], shift_ref[...])
        squares = partial_sum(r0[...] * r0[...])
        inner = partial_sum(r0[...] * w0[...])
        slope = live * (2.0 - 1.0 / (1.0 + gap_t * gap_t))
        gap_0 = own_ends(top)
        gap_other, above, below = gather_end(first)
        gap_0 = gap_0 + gap_other
        lift_0 = lift_of(slope * gap_0)
        w0[first_row] = w0[first_row] + (lift_0 - above)
        w0[last_row] = w0[last_row] - below
        inner = inner + lane_sum(top * (lift_0 - above) - bottom * below)

        gather_start(second, w0[first_row], w0[last_row], (squares, inner))
        kw0[...] = operator(w0[...], shift_ref[...])
        gap_w = own_ends(w0[first_row])
        gap_other, above, below = gather_end(second)
        gap_w = gap_w + gap_other
        lift_w = lift_of(slope * gap_w)
        totals = whole_sum(jnp.sum(slab(second)[:, q:q + 2], axis=0))
        rr, curve = totals[0:1], totals[1:2]
        alpha = rr / curve
        kw0[first_row] = kw0[first_row] - above
        kw0[last_row] = kw0[last_row] - below
        resid = r0[...] - alpha * w0[...]
        fbuf[newton, me, 0:1] = partial_sum(resid * resid)
        fbuf[newton, me, 1:2] = partial_sum(resid * w0[...])
        fbuf[newton, me, 2:3] = partial_sum(
            resid * (w0[...] - alpha * kw0[...])
        ) - alpha * lane_sum(resid[0:1] * lift_w)
        send_all(
            lambda to: fbuf.at[newton, me], fbuf.at[newton, me], fsend.at[newton], frecv.at[newton]
        )
        wait_all(fbuf.at[newton], frecv.at[newton])
        totals = whole_sum(jnp.sum(fbuf[newton, :, 0:3], axis=0))
        rr_next, cross, inner = totals[0:1], totals[1:2], totals[2:3]
        beta = rr_next / rr
        alpha_next = rr_next / (inner + 2.0 * beta * cross + beta * beta * curve)
        step_0 = alpha + alpha_next * (1.0 + beta)
        step_w = -(alpha_next * alpha)
        gap_t = gap_t + (step_0 * gap_0 + step_w * gap_w)
        top = -(
            kt[first_row] + (step_0 * (w0[first_row] - lift_0) + step_w * kw0[first_row])
        )
        bottom = -(kt[last_row] + (step_0 * w0[last_row] + step_w * kw0[last_row]))

    temp_ref[...] = temp_ref[...] + (step_0 * r0[...] + step_w * w0[...])
    final_ref[...] = kt[...] + (step_0 * w0[...] + step_w * kw0[...])
    final_ref[first_row] = lift_of(live * (2.0 * gap_t - arctan(gap_t))) - top

    for k in range(GATHERS):
        wait_all(slab(k), gsend.at[k])
        halo_copy(k).wait_send()
    wait_all(rsend_buf, rsend.at[0])
    for k in range(NEWTON):
        wait_all(fbuf.at[k], fsend.at[k])


def on_device(heat, start, shift, slave, master, d_weight, m_weight, gap_cond, active):
    n = lax.axis_size("sub")
    rows, width = heat.shape
    pairs = slave.shape[0]
    q = width // 128
    slots = pairs // 8
    listed = 2 * n * slots
    tall = (q + 2 + 7) // 8 * 8
    own_rows = (q + 7) // 8 * 8
    field = pltpu.VMEM((rows, width), jnp.float32)
    whole = lambda x: pltpu.VMEM(x.shape, x.dtype)
    sems = lambda count: pltpu.SemaphoreType.DMA((count,))
    vmem = pl.BlockSpec(memory_space=pltpu.VMEM)
    hbm = pl.BlockSpec(memory_space=pltpu.HBM)
    operands = (heat, start, shift) + tuple(
        x.reshape(1, pairs) for x in (slave, master, d_weight, m_weight, gap_cond, active)
    )
    return pl.pallas_call(
        functools.partial(kernel, n),
        out_shape=(jax.ShapeDtypeStruct((rows, width), jnp.float32),) * 2,
        in_specs=[hbm] * 9,
        out_specs=(vmem, vmem),
        scratch_shapes=[whole(x) for x in operands] + [
            pltpu.VMEM((128, listed), jnp.bfloat16),
            pltpu.VMEM((128, listed), jnp.bfloat16),
            pltpu.VMEM((own_rows, listed), jnp.float32),
            pltpu.VMEM((n * q, listed), jnp.float32),
            pltpu.VMEM((n * q, 128), jnp.float32),
            field, field, field, field,
            pltpu.VMEM((1 + NEWTON, n, q, 128), jnp.float32),
            pltpu.VMEM((NEWTON, n, tall, 128), jnp.float32),
            pltpu.VMEM((GATHERS, q, 128), jnp.float32),
            pltpu.VMEM((GATHERS, q, 128), jnp.float32),
            pltpu.VMEM((n, 8, slots), jnp.float32),
            pltpu.VMEM((n, 8, slots), jnp.float32),
            pltpu.VMEM((NEWTON, n, 4, 128), jnp.float32),
            sems(9), sems(GATHERS), sems(GATHERS), sems(GATHERS), sems(GATHERS),
            sems(1), sems(1), sems(NEWTON), sems(NEWTON),
        ],
        compiler_params=pltpu.CompilerParams(
            collective_id=0, has_side_effects=True, vmem_limit_bytes=64 * 2**20
        ),
    )(*operands)


def solution(mesh):
    field = P(("groups", "sub"), None)
    pair = P(("groups", "sub"))
    return jax.shard_map(
        on_device, mesh=mesh, in_specs=(field,) * 3 + (pair,) * 6, out_specs=(field, field),
        check_vma=False,
    )
```

```python
import functools

import jax
import jax.numpy as jnp
from jax import lax
from jax.experimental import pallas as pl
from jax.experimental.pallas import tpu as pltpu
from jax.sharding import PartitionSpec as P

NEWTON = 2
GATHERS = 1 + 2 * NEWTON
PARTS = 2
MESH = pl.DeviceIdType.MESH


def arctan(x):
    size = jnp.abs(x)
    large = size > 2.414213562373095
    middle = size > 0.4142135623730950
    top = jnp.where(large, -1.0, jnp.where(middle, size - 1.0, size))
    bottom = jnp.where(large, size, jnp.where(middle, size + 1.0, 1.0))
    base = jnp.where(large, 1.5707963267948966, jnp.where(middle, 0.7853981633974483, 0.0))
    y = top / bottom
    z = y * y
    poly = ((8.05374449538e-2 * z - 1.38776856032e-1) * z + 1.99777106478e-1) * z - 3.33329491539e-1
    result = base + (poly * z * y + y)
    return jnp.where(x < 0.0, -result, result)


def split(x, count):
    parts = []
    for _ in range(count):
        part = x.astype(jnp.bfloat16).astype(jnp.float32)
        parts.append(part)
        x = x - part
    return jnp.concatenate(parts, axis=0).astype(jnp.bfloat16)


def joined(x, count):
    rows = x.shape[0] // count
    total = x[:rows]
    for k in range(1, count):
        total = total + x[k * rows:(k + 1) * rows]
    return total


def lanes(row):
    return jnp.concatenate(
        [row[:, k * 128:(k + 1) * 128] for k in range(row.shape[1] // 128)], axis=0
    )


def flat(block):
    return jnp.concatenate([block[k:k + 1] for k in range(block.shape[0])], axis=1)


def partial_sum(x):
    x = jnp.sum(x, axis=0, keepdims=True)
    return jnp.sum(lanes(x), axis=0, keepdims=True)


def whole_sum(x):
    return jnp.sum(x, axis=1, keepdims=True)


def operator(field, shift):
    rows, width = field.shape
    row = lax.broadcasted_iota(jnp.int32, field.shape, 0)
    col = lax.broadcasted_iota(jnp.int32, field.shape, 1)
    up = jnp.where(row == 0, 0.0, pltpu.roll(field, 1, 0))
    down = jnp.where(row == rows - 1, 0.0, pltpu.roll(field, rows - 1, 0))
    left = jnp.where(col == 0, 0.0, pltpu.roll(field, 1, 1))
    right = jnp.where(col == width - 1, 0.0, pltpu.roll(field, width - 1, 1))
    return (4.0 + shift) * field - (up + down + left + right)


def kernel(
    n, heat_in, start_in, shift_in, slave_in, master_in, d_in, m_in, cond_in, active_in,
    temp_ref, final_ref,
    heat_ref, start_ref, shift_ref, slave_ref, master_ref, d_ref, m_ref, cond_ref, active_ref,
    hot_own, hot_other, pick_own, pick_other, faces, kt, r0, w0, kw0,
    plain_buf, sums_buf, hsend_buf, hrecv_buf, rsend_buf, rrecv_buf, fbuf,
    loads, gsend, grecv, hsend, hrecv, rsend, rrecv, fsend, frecv,
):
    inputs = [
        pltpu.make_async_copy(source, target, loads.at[k])
        for k, (source, target) in enumerate((
            (slave_in, slave_ref), (master_in, master_ref), (d_in, d_ref), (m_in, m_ref),
            (cond_in, cond_ref), (active_in, active_ref), (start_in, start_ref),
            (shift_in, shift_ref), (heat_in, heat_ref),
        ))
    ]
    for copy in inputs:
        copy.start()
    rows, width = heat_ref.shape
    pairs = slave_ref.shape[1]
    q = width // 128
    slots = rsend_buf.shape[2]
    listed = hot_own.shape[1]
    me = lax.axis_index("sub")
    group = lax.axis_index("groups")

    def device(j):
        return (group, lax.rem(me + j, n))

    barrier = pltpu.get_barrier_semaphore()

    def greet(j, carry):
        pl.semaphore_signal(barrier, inc=1, device_id=device(j), device_id_type=MESH)
        return carry

    lax.fori_loop(1, n, greet, 0)

    def send_all(source, target, send_sem, recv_sem):
        def send(j, carry):
            down = jnp.where(n - j > me, n - j, n - j - 1)
            up = jnp.where(j - 1 < me, j - 1, j)
            to = jnp.where(me < n // 2, down, up)
            pltpu.make_async_remote_copy(
                src_ref=source(to), dst_ref=target, send_sem=send_sem, recv_sem=recv_sem,
                device_id=(group, to), device_id_type=MESH,
            ).start()
            return carry

        lax.fori_loop(1, n, send, 0)

    def wait_all(buffer, sem):
        part = buffer.at[pl.ds(0, n - 1)]
        pltpu.make_async_copy(part, part, sem).wait()

    def records():
        slave, master = slave_ref[...], master_ref[...]
        d, m = d_ref[...], -m_ref[...]
        live = active_ref[...].astype(jnp.float32) * cond_ref[...]
        log = width.bit_length() - 1
        block = lax.broadcasted_iota(jnp.int32, (n, pairs), 0)
        upto = lax.broadcasted_iota(jnp.int32, (128, 128), 0) <= lax.broadcasted_iota(
            jnp.int32, (128, 128), 1
        )
        upto = jnp.where(upto, 1.0, 0.0).astype(jnp.bfloat16)
        slot = lax.broadcasted_iota(jnp.int32, (slots, pairs), 0)
        owners, fields, places = [], [], []
        for own, other, mine, theirs in ((slave, master, d, m), (master, slave, m, d)):
            owner = jnp.right_shift(own, log)
            named = jnp.where(block == owner, 1.0, 0.0)
            chunks = [named[:, k:k + 128] for k in range(0, pairs, 128)]
            counts = jnp.dot(
                jnp.concatenate(chunks, axis=0).astype(jnp.bfloat16), upto,
                preferred_element_type=jnp.float32,
            )
            before = jnp.zeros((n, 1), jnp.float32)
            ranks = []
            for k, chunk in enumerate(chunks):
                count = counts[k * n:(k + 1) * n] + before
                before = count[:, 127:128]
                ranks.append(jnp.sum(count * chunk, axis=0, keepdims=True) - 1.0)
            rank = jnp.concatenate(ranks, axis=1).astype(jnp.int32)
            places.append(jnp.where(slot == rank, 1.0, 0.0).astype(jnp.bfloat16))
            code = other * width + jnp.bitwise_and(own, width - 1)
            fields += [code.astype(jnp.float32), mine, theirs, live]
            owners += [owner] * 4
        fields = jnp.concatenate(fields, axis=0)[None]
        owners = jnp.concatenate(owners, axis=0)[None]
        block = lax.broadcasted_iota(jnp.int32, (n, 8, pairs), 0)
        spread = jnp.where(block == owners, fields, 0.0).reshape(8 * n, pairs)
        placed = joined(
            lax.dot_general(
                split(spread, 3), jnp.concatenate(places, axis=0), (((1,), (1,)), ((), ())),
                preferred_element_type=jnp.float32,
            ),
            3,
        )
        row = jnp.bitwise_and(lax.broadcasted_iota(jnp.int32, (8 * n, slots), 0), 7)
        placed = jnp.where(row < 4, placed[:, :slots], placed[:, slots:])
        rsend_buf[...] = placed.reshape(n, 8, slots)

    def field_of(k):
        return jnp.concatenate(
            [rrecv_buf[j, k + role:k + role + 1] for role in (0, 4) for j in range(n)], axis=1
        )

    def tables():
        code = field_of(0).astype(jnp.int32)
        own = jnp.bitwise_and(code, width - 1)
        other = jnp.right_shift(code, width.bit_length() - 1)
        node = lax.broadcasted_iota(jnp.int32, (128, listed), 0)
        for hot, face, pick, weight in (
            (hot_own, own, pick_own, field_of(1)), (hot_other, other, pick_other, field_of(2))
        ):
            low, high = jnp.bitwise_and(face, 127), jnp.right_shift(face, 7)
            nodes = jnp.where(node == low, 1.0, 0.0).astype(jnp.bfloat16)
            for k in range(PARTS):
                hot[k * 128:(k + 1) * 128] = nodes
            block = lax.broadcasted_iota(jnp.int32, pick.shape, 0)
            pick[...] = jnp.where(block == high, weight, 0.0)
        return field_of(3)

    def ends(rows_of, hot, pick):
        rows_here = rows_of.shape[0]
        parts = split(rows_of, PARTS)
        parts = jnp.concatenate(
            [parts[k * rows_here:(k + 1) * rows_here] for k in range(PARTS)], axis=1
        )
        pieces = []
        step = min(listed, 2048)
        for k in range(0, listed, step):
            here = pl.ds(k, step)
            values = jnp.dot(parts, hot[:, here], preferred_element_type=jnp.float32)
            pieces.append(jnp.sum(values * pick[:, here], axis=0, keepdims=True))
        return jnp.concatenate(pieces, axis=1)

    def lift_of(flux):
        total = joined(
            lax.dot_general(
                split(pick_own[...] * flux, PARTS), hot_own[0:128], (((1,), (1,)), ((), ())),
                preferred_element_type=jnp.float32,
            ),
            PARTS,
        )
        return flat(total[0:q])

    def slab(k):
        if k > 0 and k % 2 == 0:
            return sums_buf.at[k // 2 - 1]
        return plain_buf.at[(k + 1) // 2]

    def gather_start(k, top, bottom, partials=()):
        buffer = slab(k)
        buffer[me, 0:q] = lanes(top)
        for place, partial in enumerate(partials):
            buffer[me, q + place:q + place + 1] = partial
        hsend_buf[k] = lanes(bottom)
        send_all(lambda to: buffer.at[me], buffer.at[me], gsend.at[k], grecv.at[k])
        halo_copy(k).start()

    def halo_copy(k):
        return pltpu.make_async_remote_copy(
            src_ref=hsend_buf.at[k], dst_ref=hrecv_buf.at[k], send_sem=hsend.at[k],
            recv_sem=hrecv.at[k], device_id=device(1), device_id_type=MESH,
        )

    def own_ends(top):
        own = jnp.concatenate(
            [lanes(top), jnp.zeros((pick_own.shape[0] - q, 128), jnp.float32)], axis=0
        )
        return ends(own, hot_own, pick_own)

    def gather_end(k):
        buffer = slab(k)
        wait_all(buffer, grecv.at[k])
        halo_copy(k).wait_recv()
        for j in range(n):
            faces[j * q:(j + 1) * q] = buffer[j, 0:q]
        above = jnp.where(me == 0, 0.0, flat(hrecv_buf[k]))
        below = jnp.where(me == n - 1, 0.0, flat(buffer[lax.rem(me + 1, n), 0:q]))
        return ends(faces[...], hot_other, pick_other), above, below

    def lane_sum(row):
        return jnp.sum(lanes(row), axis=0, keepdims=True)

    first_row, last_row = pl.ds(0, 1), pl.ds(rows - 1, 1)

    for copy in inputs[:6]:
        copy.wait()
    records()
    inputs[6].wait()
    pl.semaphore_wait(barrier, n - 1)
    send_all(lambda to: rsend_buf.at[to], rrecv_buf.at[me], rsend.at[0], rrecv.at[0])
    gather_start(0, start_ref[first_row], start_ref[last_row])
    rrecv_buf[me] = rsend_buf[me]
    inputs[7].wait()
    inputs[8].wait()
    kt[...] = operator(start_ref[...], shift_ref[...]) - heat_ref[...]
    wait_all(rrecv_buf, rrecv.at[0])
    live = tables()
    gap_t = own_ends(start_ref[first_row])
    gap_other, above, below = gather_end(0)
    gap_t = gap_t + gap_other
    kt[first_row] = kt[first_row] - above
    kt[last_row] = kt[last_row] - below
    top, bottom = -kt[first_row], -kt[last_row]

    for newton in range(NEWTON):
        first, second = 1 + 2 * newton, 2 + 2 * newton
        top = top - lift_of(live * (2.0 * gap_t - arctan(gap_t)))
        gather_start(first, top, bottom)
        if newton > 0:
            kt[...] = kt[...] + (step_0 * w0[...] + step_w * kw0[...])
            kt[first_row] = kt[first_row] - step_0 * lift_0
            temp_ref[...] = temp_ref[...] + (step_0 * r0[...] + step_w * w0[...])
        else:
            temp_ref[...] = start_ref[...]
        r0[...] = -kt[...]
        r0[first_row] = top
        r0[last_row] = bottom
        w0[...] = operator(r0[...], shift_ref[...])
        squares = partial_sum(r0[...] * r0[...])
        inner = partial_sum(r0[...] * w0[...])
        slope = live * (2.0 - 1.0 / (1.0 + gap_t * gap_t))
        gap_0 = own_ends(top)
        gap_other, above, below = gather_end(first)
        gap_0 = gap_0 + gap_other
        lift_0 = lift_of(slope * gap_0)
        w0[first_row] = w0[first_row] + (lift_0 - above)
        w0[last_row] = w0[last_row] - below
        inner = inner + lane_sum(top * (lift_0 - above) - bottom * below)

        gather_start(second, w0[first_row], w0[last_row], (squares, inner))
        kw0[...] = operator(w0[...], shift_ref[...])
        gap_w = own_ends(w0[first_row])
        gap_other, above, below = gather_end(second)
        gap_w = gap_w + gap_other
        lift_w = lift_of(slope * gap_w)
        totals = whole_sum(jnp.sum(slab(second)[:, q:q + 2], axis=0))
        rr, curve = totals[0:1], totals[1:2]
        alpha = rr / curve
        kw0[first_row] = kw0[first_row] - above
        kw0[last_row] = kw0[last_row] - below
        resid = r0[...] - alpha * w0[...]
        fbuf[newton, me, 0:1] = partial_sum(resid * resid)
        fbuf[newton, me, 1:2] = partial_sum(resid * w0[...])
        fbuf[newton, me, 2:3] = partial_sum(
            resid * (w0[...] - alpha * kw0[...])
        ) - alpha * lane_sum(resid[0:1] * lift_w)
        send_all(
            lambda to: fbuf.at[newton, me], fbuf.at[newton, me], fsend.at[newton], frecv.at[newton]
        )
        wait_all(fbuf.at[newton], frecv.at[newton])
        totals = whole_sum(jnp.sum(fbuf[newton, :, 0:3], axis=0))
        rr_next, cross, inner = totals[0:1], totals[1:2], totals[2:3]
        beta = rr_next / rr
        alpha_next = rr_next / (inner + 2.0 * beta * cross + beta * beta * curve)
        step_0 = alpha + alpha_next * (1.0 + beta)
        step_w = -(alpha_next * alpha)
        gap_t = gap_t + (step_0 * gap_0 + step_w * gap_w)
        top = -(
            kt[first_row] + (step_0 * (w0[first_row] - lift_0) + step_w * kw0[first_row])
        )
        bottom = -(kt[last_row] + (step_0 * w0[last_row] + step_w * kw0[last_row]))

    temp_ref[...] = temp_ref[...] + (step_0 * r0[...] + step_w * w0[...])
    final_ref[...] = kt[...] + (step_0 * w0[...] + step_w * kw0[...])
    final_ref[first_row] = lift_of(live * (2.0 * gap_t - arctan(gap_t))) - top

    for k in range(GATHERS):
        wait_all(slab(k), gsend.at[k])
        halo_copy(k).wait_send()
    wait_all(rsend_buf, rsend.at[0])
    for k in range(NEWTON):
        wait_all(fbuf.at[k], fsend.at[k])


def on_device(heat, start, shift, slave, master, d_weight, m_weight, gap_cond, active):
    n = lax.axis_size("sub")
    rows, width = heat.shape
    pairs = slave.shape[0]
    q = width // 128
    slots = pairs // 8
    listed = 2 * n * slots
    tall = (q + 2 + 7) // 8 * 8
    own_rows = (q + 15) // 16 * 16
    field = pltpu.VMEM((rows, width), jnp.float32)
    whole = lambda x: pltpu.VMEM(x.shape, x.dtype)
    sems = lambda count: pltpu.SemaphoreType.DMA((count,))
    vmem = pl.BlockSpec(memory_space=pltpu.VMEM)
    hbm = pl.BlockSpec(memory_space=pltpu.HBM)
    operands = (heat, start, shift) + tuple(
        x.reshape(1, pairs) for x in (slave, master, d_weight, m_weight, gap_cond, active)
    )
    return pl.pallas_call(
        functools.partial(kernel, n),
        out_shape=(jax.ShapeDtypeStruct((rows, width), jnp.float32),) * 2,
        in_specs=[hbm] * 9,
        out_specs=(vmem, vmem),
        scratch_shapes=[whole(x) for x in operands] + [
            pltpu.VMEM((PARTS * 128, listed), jnp.bfloat16),
            pltpu.VMEM((PARTS * 128, listed), jnp.bfloat16),
            pltpu.VMEM((own_rows, listed), jnp.float32),
            pltpu.VMEM((n * q, listed), jnp.float32),
            pltpu.VMEM((n * q, 128), jnp.float32),
            field, field, field, field,
            pltpu.VMEM((1 + NEWTON, n, q, 128), jnp.float32),
            pltpu.VMEM((NEWTON, n, tall, 128), jnp.float32),
            pltpu.VMEM((GATHERS, q, 128), jnp.float32),
            pltpu.VMEM((GATHERS, q, 128), jnp.float32),
            pltpu.VMEM((n, 8, slots), jnp.float32),
            pltpu.VMEM((n, 8, slots), jnp.float32),
            pltpu.VMEM((NEWTON, n, 4, 128), jnp.float32),
            sems(9), sems(GATHERS), sems(GATHERS), sems(GATHERS), sems(GATHERS),
            sems(1), sems(1), sems(NEWTON), sems(NEWTON),
        ],
        compiler_params=pltpu.CompilerParams(
            collective_id=0, has_side_effects=True, vmem_limit_bytes=64 * 2**20
        ),
    )(*operands)


def solution(mesh):
    field = P(("groups", "sub"), None)
    pair = P(("groups", "sub"))
    return jax.shard_map(
        on_device, mesh=mesh, in_specs=(field,) * 3 + (pair,) * 6, out_specs=(field, field),
        check_vma=False,
    )
```

```python
import functools

import jax
import jax.numpy as jnp
from jax import lax
from jax.experimental import pallas as pl
from jax.experimental.pallas import tpu as pltpu
from jax.sharding import PartitionSpec as P

NEWTON = 2
GATHERS = 1 + 2 * NEWTON
PARTS = 2
MESH = pl.DeviceIdType.MESH


def arctan(x):
    size = jnp.abs(x)
    large = size > 2.414213562373095
    middle = size > 0.4142135623730950
    top = jnp.where(large, -1.0, jnp.where(middle, size - 1.0, size))
    bottom = jnp.where(large, size, jnp.where(middle, size + 1.0, 1.0))
    base = jnp.where(large, 1.5707963267948966, jnp.where(middle, 0.7853981633974483, 0.0))
    y = top / bottom
    z = y * y
    poly = ((8.05374449538e-2 * z - 1.38776856032e-1) * z + 1.99777106478e-1) * z - 3.33329491539e-1
    result = base + (poly * z * y + y)
    return jnp.where(x < 0.0, -result, result)


def split(x, count):
    parts = []
    for _ in range(count):
        part = x.astype(jnp.bfloat16).astype(jnp.float32)
        parts.append(part)
        x = x - part
    return jnp.concatenate(parts, axis=0).astype(jnp.bfloat16)


def joined(x, count):
    rows = x.shape[0] // count
    total = x[:rows]
    for k in range(1, count):
        total = total + x[k * rows:(k + 1) * rows]
    return total


def lanes(row):
    return jnp.concatenate(
        [row[:, k * 128:(k + 1) * 128] for k in range(row.shape[1] // 128)], axis=0
    )


def flat(block):
    return jnp.concatenate([block[k:k + 1] for k in range(block.shape[0])], axis=1)


def partial_sum(x):
    x = jnp.sum(x, axis=0, keepdims=True)
    return jnp.sum(lanes(x), axis=0, keepdims=True)


def whole_sum(x):
    return jnp.sum(x, axis=1, keepdims=True)


def operator(field, shift):
    rows, width = field.shape
    row = lax.broadcasted_iota(jnp.int32, field.shape, 0)
    col = lax.broadcasted_iota(jnp.int32, field.shape, 1)
    up = jnp.where(row == 0, 0.0, pltpu.roll(field, 1, 0))
    down = jnp.where(row == rows - 1, 0.0, pltpu.roll(field, rows - 1, 0))
    left = jnp.where(col == 0, 0.0, pltpu.roll(field, 1, 1))
    right = jnp.where(col == width - 1, 0.0, pltpu.roll(field, width - 1, 1))
    return (4.0 + shift) * field - (up + down + left + right)


def kernel(
    n, heat_in, start_in, shift_in, slave_in, master_in, d_in, m_in, cond_in, active_in,
    temp_out, final_out,
    temp_ref, final_ref, heat_ref, start_ref, shift_ref, slave_ref, master_ref, d_ref, m_ref, cond_ref, active_ref,
    hot_own, hot_other, pick_own, pick_other, faces, kt, r0, w0, kw0,
    plain_buf, sums_buf, hsend_buf, hrecv_buf, rsend_buf, rrecv_buf, fbuf,
    loads, stores, gsend, grecv, hsend, hrecv, rsend, rrecv, fsend, frecv,
):
    inputs = [
        pltpu.make_async_copy(source, target, loads.at[k])
        for k, (source, target) in enumerate((
            (slave_in, slave_ref), (master_in, master_ref), (d_in, d_ref), (m_in, m_ref),
            (cond_in, cond_ref), (active_in, active_ref), (start_in, start_ref),
            (shift_in, shift_ref), (heat_in, heat_ref),
        ))
    ]
    for copy in inputs:
        copy.start()
    rows, width = heat_ref.shape
    pairs = slave_ref.shape[1]
    q = width // 128
    slots = rsend_buf.shape[2]
    listed = hot_own.shape[1]
    me = lax.axis_index("sub")
    group = lax.axis_index("groups")

    def device(j):
        return (group, lax.rem(me + j, n))

    barrier = pltpu.get_barrier_semaphore()

    def greet(j, carry):
        pl.semaphore_signal(barrier, inc=1, device_id=device(j), device_id_type=MESH)
        return carry

    lax.fori_loop(1, n, greet, 0)

    def send_all(source, target, send_sem, recv_sem):
        def send(j, carry):
            down = jnp.where(n - j > me, n - j, n - j - 1)
            up = jnp.where(j - 1 < me, j - 1, j)
            to = jnp.where(me < n // 2, down, up)
            pltpu.make_async_remote_copy(
                src_ref=source(to), dst_ref=target, send_sem=send_sem, recv_sem=recv_sem,
                device_id=(group, to), device_id_type=MESH,
            ).start()
            return carry

        lax.fori_loop(1, n, send, 0)

    def wait_all(buffer, sem):
        part = buffer.at[pl.ds(0, n - 1)]
        pltpu.make_async_copy(part, part, sem).wait()

    def records():
        slave, master = slave_ref[...], master_ref[...]
        d, m = d_ref[...], -m_ref[...]
        live = active_ref[...].astype(jnp.float32) * cond_ref[...]
        log = width.bit_length() - 1
        block = lax.broadcasted_iota(jnp.int32, (n, pairs), 0)
        upto = lax.broadcasted_iota(jnp.int32, (128, 128), 0) <= lax.broadcasted_iota(
            jnp.int32, (128, 128), 1
        )
        upto = jnp.where(upto, 1.0, 0.0).astype(jnp.bfloat16)
        slot = lax.broadcasted_iota(jnp.int32, (slots, pairs), 0)
        owners, fields, places = [], [], []
        for own, other, mine, theirs in ((slave, master, d, m), (master, slave, m, d)):
            owner = jnp.right_shift(own, log)
            named = jnp.where(block == owner, 1.0, 0.0)
            chunks = [named[:, k:k + 128] for k in range(0, pairs, 128)]
            counts = jnp.dot(
                jnp.concatenate(chunks, axis=0).astype(jnp.bfloat16), upto,
                preferred_element_type=jnp.float32,
            )
            before = jnp.zeros((n, 1), jnp.float32)
            ranks = []
            for k, chunk in enumerate(chunks):
                count = counts[k * n:(k + 1) * n] + before
                before = count[:, 127:128]
                ranks.append(jnp.sum(count * chunk, axis=0, keepdims=True) - 1.0)
            rank = jnp.concatenate(ranks, axis=1).astype(jnp.int32)
            places.append(jnp.where(slot == rank, 1.0, 0.0).astype(jnp.bfloat16))
            code = other * width + jnp.bitwise_and(own, width - 1)
            fields += [code.astype(jnp.float32), mine, theirs, live]
            owners += [owner] * 4
        fields = jnp.concatenate(fields, axis=0)[None]
        owners = jnp.concatenate(owners, axis=0)[None]
        block = lax.broadcasted_iota(jnp.int32, (n, 8, pairs), 0)
        spread = jnp.where(block == owners, fields, 0.0).reshape(8 * n, pairs)
        placed = joined(
            lax.dot_general(
                split(spread, 3), jnp.concatenate(places, axis=0), (((1,), (1,)), ((), ())),
                preferred_element_type=jnp.float32,
            ),
            3,
        )
        row = jnp.bitwise_and(lax.broadcasted_iota(jnp.int32, (8 * n, slots), 0), 7)
        placed = jnp.where(row < 4, placed[:, :slots], placed[:, slots:])
        rsend_buf[...] = placed.reshape(n, 8, slots)

    def field_of(k):
        return jnp.concatenate(
            [rrecv_buf[j, k + role:k + role + 1] for role in (0, 4) for j in range(n)], axis=1
        )

    def tables():
        code = field_of(0).astype(jnp.int32)
        own = jnp.bitwise_and(code, width - 1)
        other = jnp.right_shift(code, width.bit_length() - 1)
        node = lax.broadcasted_iota(jnp.int32, (128, listed), 0)
        for hot, face, pick, weight in (
            (hot_own, own, pick_own, field_of(1)), (hot_other, other, pick_other, field_of(2))
        ):
            low, high = jnp.bitwise_and(face, 127), jnp.right_shift(face, 7)
            nodes = jnp.where(node == low, 1.0, 0.0).astype(jnp.bfloat16)
            for k in range(PARTS):
                hot[k * 128:(k + 1) * 128] = nodes
            block = lax.broadcasted_iota(jnp.int32, pick.shape, 0)
            pick[...] = jnp.where(block == high, weight, 0.0)
        return field_of(3)

    def ends(rows_of, hot, pick):
        rows_here = rows_of.shape[0]
        parts = split(rows_of, PARTS)
        parts = jnp.concatenate(
            [parts[k * rows_here:(k + 1) * rows_here] for k in range(PARTS)], axis=1
        )
        pieces = []
        step = min(listed, 2048)
        for k in range(0, listed, step):
            here = pl.ds(k, step)
            values = jnp.dot(parts, hot[:, here], preferred_element_type=jnp.float32)
            pieces.append(jnp.sum(values * pick[:, here], axis=0, keepdims=True))
        return jnp.concatenate(pieces, axis=1)

    def lift_of(flux):
        total = joined(
            lax.dot_general(
                split(pick_own[...] * flux, PARTS), hot_own[0:128], (((1,), (1,)), ((), ())),
                preferred_element_type=jnp.float32,
            ),
            PARTS,
        )
        return flat(total[0:q])

    def slab(k):
        if k > 0 and k % 2 == 0:
            return sums_buf.at[k // 2 - 1]
        return plain_buf.at[(k + 1) // 2]

    def gather_start(k, top, bottom, partials=()):
        buffer = slab(k)
        buffer[me, 0:q] = lanes(top)
        for place, partial in enumerate(partials):
            buffer[me, q + place:q + place + 1] = partial
        hsend_buf[k] = lanes(bottom)
        send_all(lambda to: buffer.at[me], buffer.at[me], gsend.at[k], grecv.at[k])
        halo_copy(k).start()

    def halo_copy(k):
        return pltpu.make_async_remote_copy(
            src_ref=hsend_buf.at[k], dst_ref=hrecv_buf.at[k], send_sem=hsend.at[k],
            recv_sem=hrecv.at[k], device_id=device(1), device_id_type=MESH,
        )

    def own_ends(top):
        own = jnp.concatenate(
            [lanes(top), jnp.zeros((pick_own.shape[0] - q, 128), jnp.float32)], axis=0
        )
        return ends(own, hot_own, pick_own)

    def gather_end(k):
        buffer = slab(k)
        wait_all(buffer, grecv.at[k])
        halo_copy(k).wait_recv()
        for j in range(n):
            faces[j * q:(j + 1) * q] = buffer[j, 0:q]
        above = jnp.where(me == 0, 0.0, flat(hrecv_buf[k]))
        below = jnp.where(me == n - 1, 0.0, flat(buffer[lax.rem(me + 1, n), 0:q]))
        return ends(faces[...], hot_other, pick_other), above, below

    def lane_sum(row):
        return jnp.sum(lanes(row), axis=0, keepdims=True)

    first_row, last_row = pl.ds(0, 1), pl.ds(rows - 1, 1)

    for copy in inputs[:6]:
        copy.wait()
    records()
    inputs[6].wait()
    pl.semaphore_wait(barrier, n - 1)
    send_all(lambda to: rsend_buf.at[to], rrecv_buf.at[me], rsend.at[0], rrecv.at[0])
    gather_start(0, start_ref[first_row], start_ref[last_row])
    rrecv_buf[me] = rsend_buf[me]
    inputs[7].wait()
    inputs[8].wait()
    kt[...] = operator(start_ref[...], shift_ref[...]) - heat_ref[...]
    wait_all(rrecv_buf, rrecv.at[0])
    live = tables()
    gap_t = own_ends(start_ref[first_row])
    gap_other, above, below = gather_end(0)
    gap_t = gap_t + gap_other
    kt[first_row] = kt[first_row] - above
    kt[last_row] = kt[last_row] - below
    top, bottom = -kt[first_row], -kt[last_row]

    for newton in range(NEWTON):
        first, second = 1 + 2 * newton, 2 + 2 * newton
        top = top - lift_of(live * (2.0 * gap_t - arctan(gap_t)))
        gather_start(first, top, bottom)
        if newton > 0:
            kt[...] = kt[...] + (step_0 * w0[...] + step_w * kw0[...])
            kt[first_row] = kt[first_row] - step_0 * lift_0
            temp_ref[...] = temp_ref[...] + (step_0 * r0[...] + step_w * w0[...])
        else:
            temp_ref[...] = start_ref[...]
        r0[...] = -kt[...]
        r0[first_row] = top
        r0[last_row] = bottom
        w0[...] = operator(r0[...], shift_ref[...])
        squares = partial_sum(r0[...] * r0[...])
        inner = partial_sum(r0[...] * w0[...])
        slope = live * (2.0 - 1.0 / (1.0 + gap_t * gap_t))
        gap_0 = own_ends(top)
        gap_other, above, below = gather_end(first)
        gap_0 = gap_0 + gap_other
        lift_0 = lift_of(slope * gap_0)
        w0[first_row] = w0[first_row] + (lift_0 - above)
        w0[last_row] = w0[last_row] - below
        inner = inner + lane_sum(top * (lift_0 - above) - bottom * below)

        gather_start(second, w0[first_row], w0[last_row], (squares, inner))
        kw0[...] = operator(w0[...], shift_ref[...])
        gap_w = own_ends(w0[first_row])
        gap_other, above, below = gather_end(second)
        gap_w = gap_w + gap_other
        lift_w = lift_of(slope * gap_w)
        totals = whole_sum(jnp.sum(slab(second)[:, q:q + 2], axis=0))
        rr, curve = totals[0:1], totals[1:2]
        alpha = rr / curve
        kw0[first_row] = kw0[first_row] - above
        kw0[last_row] = kw0[last_row] - below
        resid = r0[...] - alpha * w0[...]
        fbuf[newton, me, 0:1] = partial_sum(resid * resid)
        fbuf[newton, me, 1:2] = partial_sum(resid * w0[...])
        fbuf[newton, me, 2:3] = partial_sum(
            resid * (w0[...] - alpha * kw0[...])
        ) - alpha * lane_sum(resid[0:1] * lift_w)
        send_all(
            lambda to: fbuf.at[newton, me], fbuf.at[newton, me], fsend.at[newton], frecv.at[newton]
        )
        wait_all(fbuf.at[newton], frecv.at[newton])
        totals = whole_sum(jnp.sum(fbuf[newton, :, 0:3], axis=0))
        rr_next, cross, inner = totals[0:1], totals[1:2], totals[2:3]
        beta = rr_next / rr
        alpha_next = rr_next / (inner + 2.0 * beta * cross + beta * beta * curve)
        step_0 = alpha + alpha_next * (1.0 + beta)
        step_w = -(alpha_next * alpha)
        gap_t = gap_t + (step_0 * gap_0 + step_w * gap_w)
        top = -(
            kt[first_row] + (step_0 * (w0[first_row] - lift_0) + step_w * kw0[first_row])
        )
        bottom = -(kt[last_row] + (step_0 * w0[last_row] + step_w * kw0[last_row]))

    temp_ref[...] = temp_ref[...] + (step_0 * r0[...] + step_w * w0[...])
    outputs = [
        pltpu.make_async_copy(temp_ref, temp_out, stores.at[0]),
        pltpu.make_async_copy(final_ref, final_out, stores.at[1]),
    ]
    outputs[0].start()
    final_ref[...] = kt[...] + (step_0 * w0[...] + step_w * kw0[...])
    final_ref[first_row] = lift_of(live * (2.0 * gap_t - arctan(gap_t))) - top
    outputs[1].start()

    for k in range(GATHERS):
        wait_all(slab(k), gsend.at[k])
        halo_copy(k).wait_send()
    wait_all(rsend_buf, rsend.at[0])
    for k in range(NEWTON):
        wait_all(fbuf.at[k], fsend.at[k])
    for copy in outputs:
        copy.wait()


def settle(first_in, second_in, first_out, second_out, hold, loads, stores):
    count, height = hold.shape[0] // 2, hold.shape[1]
    moves = []
    for k in range(2 * count):
        source = (first_in, second_in)[k // count]
        target = (first_out, second_out)[k // count]
        here = pl.ds(k % count * height, height)
        moves.append((
            pltpu.make_async_copy(source.at[here], hold.at[k], loads.at[k]),
            pltpu.make_async_copy(hold.at[k], target.at[here], stores.at[k]),
        ))
    for load, _ in moves:
        load.start()
    for load, store in moves:
        load.wait()
        store.start()
    for _, store in moves:
        store.wait()


def on_device(heat, start, shift, slave, master, d_weight, m_weight, gap_cond, active):
    n = lax.axis_size("sub")
    rows, width = heat.shape
    pairs = slave.shape[0]
    q = width // 128
    slots = pairs // 8
    listed = 2 * n * slots
    tall = (q + 2 + 7) // 8 * 8
    own_rows = (q + 15) // 16 * 16
    field = pltpu.VMEM((rows, width), jnp.float32)
    whole = lambda x: pltpu.VMEM(x.shape, x.dtype)
    sems = lambda count: pltpu.SemaphoreType.DMA((count,))
    hbm = pl.BlockSpec(memory_space=pltpu.HBM)
    operands = (heat, start, shift) + tuple(
        x.reshape(1, pairs) for x in (slave, master, d_weight, m_weight, gap_cond, active)
    )
    results = pl.pallas_call(
        functools.partial(kernel, n),
        out_shape=(jax.ShapeDtypeStruct((rows, width), jnp.float32),) * 2,
        in_specs=[hbm] * 9,
        out_specs=(hbm, hbm),
        scratch_shapes=[field, field] + [whole(x) for x in operands] + [
            pltpu.VMEM((PARTS * 128, listed), jnp.bfloat16),
            pltpu.VMEM((PARTS * 128, listed), jnp.bfloat16),
            pltpu.VMEM((own_rows, listed), jnp.float32),
            pltpu.VMEM((n * q, listed), jnp.float32),
            pltpu.VMEM((n * q, 128), jnp.float32),
            field, field, field, field,
            pltpu.VMEM((1 + NEWTON, n, q, 128), jnp.float32),
            pltpu.VMEM((NEWTON, n, tall, 128), jnp.float32),
            pltpu.VMEM((GATHERS, q, 128), jnp.float32),
            pltpu.VMEM((GATHERS, q, 128), jnp.float32),
            pltpu.VMEM((n, 8, slots), jnp.float32),
            pltpu.VMEM((n, 8, slots), jnp.float32),
            pltpu.VMEM((NEWTON, n, 4, 128), jnp.float32),
            sems(9), sems(2), sems(GATHERS), sems(GATHERS), sems(GATHERS), sems(GATHERS),
            sems(1), sems(1), sems(NEWTON), sems(NEWTON),
        ],
        compiler_params=pltpu.CompilerParams(
            collective_id=0, has_side_effects=True, vmem_limit_bytes=64 * 2**20
        ),
    )(*operands)
    pieces = 4
    return pl.pallas_call(
        settle,
        out_shape=(jax.ShapeDtypeStruct((rows, width), jnp.float32),) * 2,
        in_specs=[hbm] * 2,
        out_specs=(hbm, hbm),
        scratch_shapes=[
            pltpu.VMEM((2 * pieces, rows // pieces, width), jnp.float32),
            sems(2 * pieces), sems(2 * pieces),
        ],
        compiler_params=pltpu.CompilerParams(vmem_limit_bytes=64 * 2**20),
    )(*results)


def solution(mesh):
    field = P(("groups", "sub"), None)
    pair = P(("groups", "sub"))
    return jax.shard_map(
        on_device, mesh=mesh, in_specs=(field,) * 3 + (pair,) * 6, out_specs=(field, field),
        check_vma=False,
    )
```

```python
import functools

import jax
import jax.numpy as jnp
from jax import lax
from jax.experimental import pallas as pl
from jax.experimental.pallas import tpu as pltpu
from jax.sharding import PartitionSpec as P

NEWTON = 2
GATHERS = 1 + 2 * NEWTON
PARTS = 2
MESH = pl.DeviceIdType.MESH


def arctan(x):
    size = jnp.abs(x)
    large = size > 2.414213562373095
    middle = size > 0.4142135623730950
    top = jnp.where(large, -1.0, jnp.where(middle, size - 1.0, size))
    bottom = jnp.where(large, size, jnp.where(middle, size + 1.0, 1.0))
    base = jnp.where(large, 1.5707963267948966, jnp.where(middle, 0.7853981633974483, 0.0))
    y = top / bottom
    z = y * y
    poly = ((8.05374449538e-2 * z - 1.38776856032e-1) * z + 1.99777106478e-1) * z - 3.33329491539e-1
    result = base + (poly * z * y + y)
    return jnp.where(x < 0.0, -result, result)


def split(x, count):
    parts = []
    for _ in range(count):
        part = x.astype(jnp.bfloat16).astype(jnp.float32)
        parts.append(part)
        x = x - part
    return jnp.concatenate(parts, axis=0).astype(jnp.bfloat16)


def joined(x, count):
    rows = x.shape[0] // count
    total = x[:rows]
    for k in range(1, count):
        total = total + x[k * rows:(k + 1) * rows]
    return total


def lanes(row):
    return jnp.concatenate(
        [row[:, k * 128:(k + 1) * 128] for k in range(row.shape[1] // 128)], axis=0
    )


def flat(block):
    return jnp.concatenate([block[k:k + 1] for k in range(block.shape[0])], axis=1)


def partial_sum(x):
    x = jnp.sum(x, axis=0, keepdims=True)
    return jnp.sum(lanes(x), axis=0, keepdims=True)


def whole_sum(x):
    return jnp.sum(x, axis=1, keepdims=True)


def operator(field, shift):
    rows, width = field.shape
    row = lax.broadcasted_iota(jnp.int32, field.shape, 0)
    col = lax.broadcasted_iota(jnp.int32, field.shape, 1)
    up = jnp.where(row == 0, 0.0, pltpu.roll(field, 1, 0))
    down = jnp.where(row == rows - 1, 0.0, pltpu.roll(field, rows - 1, 0))
    left = jnp.where(col == 0, 0.0, pltpu.roll(field, 1, 1))
    right = jnp.where(col == width - 1, 0.0, pltpu.roll(field, width - 1, 1))
    return (4.0 + shift) * field - (up + down + left + right)


def kernel(
    n, heat_in, start_in, shift_in, slave_in, master_in, d_in, m_in, cond_in, active_in,
    temp_out, final_out,
    temp_ref, final_ref, heat_ref, start_ref, shift_ref, slave_ref, master_ref, d_ref, m_ref, cond_ref, active_ref,
    hot_own, hot_other, hot_back, pick_own, pick_other, faces, kt, r0, w0, kw0,
    plain_buf, sums_buf, hsend_buf, hrecv_buf, rsend_buf, rrecv_buf, fbuf,
    loads, stores, gsend, grecv, hsend, hrecv, rsend, rrecv, fsend, frecv,
):
    inputs = [
        pltpu.make_async_copy(source, target, loads.at[k])
        for k, (source, target) in enumerate((
            (slave_in, slave_ref), (master_in, master_ref), (d_in, d_ref), (m_in, m_ref),
            (cond_in, cond_ref), (active_in, active_ref), (start_in, start_ref),
            (shift_in, shift_ref), (heat_in, heat_ref),
        ))
    ]
    for copy in inputs:
        copy.start()
    rows, width = heat_ref.shape
    pairs = slave_ref.shape[1]
    q = width // 128
    slots = rsend_buf.shape[2]
    lifted = (q + 7) // 8 * 8
    listed = hot_own.shape[1]
    me = lax.axis_index("sub")
    group = lax.axis_index("groups")

    def device(j):
        return (group, lax.rem(me + j, n))

    barrier = pltpu.get_barrier_semaphore()

    def greet(j, carry):
        pl.semaphore_signal(barrier, inc=1, device_id=device(j), device_id_type=MESH)
        return carry

    lax.fori_loop(1, n, greet, 0)

    def send_all(source, target, send_sem, recv_sem):
        def send(j, carry):
            down = jnp.where(n - j > me, n - j, n - j - 1)
            up = jnp.where(j - 1 < me, j - 1, j)
            to = jnp.where(me < n // 2, down, up)
            pltpu.make_async_remote_copy(
                src_ref=source(to), dst_ref=target, send_sem=send_sem, recv_sem=recv_sem,
                device_id=(group, to), device_id_type=MESH,
            ).start()
            return carry

        lax.fori_loop(1, n, send, 0)

    def wait_all(buffer, sem):
        part = buffer.at[pl.ds(0, n - 1)]
        pltpu.make_async_copy(part, part, sem).wait()

    def records():
        slave, master = slave_ref[...], master_ref[...]
        d, m = d_ref[...], -m_ref[...]
        live = active_ref[...].astype(jnp.float32) * cond_ref[...]
        log = width.bit_length() - 1
        block = lax.broadcasted_iota(jnp.int32, (n, pairs), 0)
        upto = lax.broadcasted_iota(jnp.int32, (128, 128), 0) <= lax.broadcasted_iota(
            jnp.int32, (128, 128), 1
        )
        upto = jnp.where(upto, 1.0, 0.0).astype(jnp.bfloat16)
        slot = lax.broadcasted_iota(jnp.int32, (slots, pairs), 0)
        owners, fields, places = [], [], []
        for own, other, mine, theirs in ((slave, master, d, m), (master, slave, m, d)):
            owner = jnp.right_shift(own, log)
            named = jnp.where(block == owner, 1.0, 0.0)
            chunks = [named[:, k:k + 128] for k in range(0, pairs, 128)]
            counts = jnp.dot(
                jnp.concatenate(chunks, axis=0).astype(jnp.bfloat16), upto,
                preferred_element_type=jnp.float32,
            )
            before = jnp.zeros((n, 1), jnp.float32)
            ranks = []
            for k, chunk in enumerate(chunks):
                count = counts[k * n:(k + 1) * n] + before
                before = count[:, 127:128]
                ranks.append(jnp.sum(count * chunk, axis=0, keepdims=True) - 1.0)
            rank = jnp.concatenate(ranks, axis=1).astype(jnp.int32)
            places.append(jnp.where(slot == rank, 1.0, 0.0).astype(jnp.bfloat16))
            code = other * width + jnp.bitwise_and(own, width - 1)
            fields += [code.astype(jnp.float32), mine, theirs, live]
            owners += [owner] * 4
        fields = jnp.concatenate(fields, axis=0)[None]
        owners = jnp.concatenate(owners, axis=0)[None]
        block = lax.broadcasted_iota(jnp.int32, (n, 8, pairs), 0)
        spread = jnp.where(block == owners, fields, 0.0).reshape(8 * n, pairs)
        placed = joined(
            lax.dot_general(
                split(spread, 3), jnp.concatenate(places, axis=0), (((1,), (1,)), ((), ())),
                preferred_element_type=jnp.float32,
            ),
            3,
        )
        row = jnp.bitwise_and(lax.broadcasted_iota(jnp.int32, (8 * n, slots), 0), 7)
        placed = jnp.where(row < 4, placed[:, :slots], placed[:, slots:])
        rsend_buf[...] = placed.reshape(n, 8, slots)

    def field_of(k):
        return jnp.concatenate(
            [rrecv_buf[j, k + role:k + role + 1] for role in (0, 4) for j in range(n)], axis=1
        )

    def tables():
        code = field_of(0).astype(jnp.int32)
        own = jnp.bitwise_and(code, width - 1)
        other = jnp.right_shift(code, width.bit_length() - 1)
        node = lax.broadcasted_iota(jnp.int32, (128, listed), 0)
        for hot, face, pick, weight in (
            (hot_own, own, pick_own, field_of(1)), (hot_other, other, pick_other, field_of(2))
        ):
            low, high = jnp.bitwise_and(face, 127), jnp.right_shift(face, 7)
            nodes = jnp.where(node == low, 1.0, 0.0).astype(jnp.bfloat16)
            for k in range(PARTS):
                hot[k * 128:(k + 1) * 128] = nodes
            block = lax.broadcasted_iota(jnp.int32, pick.shape, 0)
            pick[...] = jnp.where(block == high, weight, 0.0)
        hot_back[...] = hot_own[0:128].T
        return field_of(3)

    def ends(rows_of, hot, pick):
        rows_here = rows_of.shape[0]
        parts = split(rows_of, PARTS)
        parts = jnp.concatenate(
            [parts[k * rows_here:(k + 1) * rows_here] for k in range(PARTS)], axis=1
        )
        pieces = []
        step = min(listed, 2048)
        for k in range(0, listed, step):
            here = pl.ds(k, step)
            values = jnp.dot(parts, hot[:, here], preferred_element_type=jnp.float32)
            pieces.append(jnp.sum(values * pick[:, here], axis=0, keepdims=True))
        return jnp.concatenate(pieces, axis=1)

    def lift_of(flux):
        total = joined(
            jnp.dot(
                split(pick_own[0:lifted] * flux, PARTS), hot_back[...],
                preferred_element_type=jnp.float32,
            ),
            PARTS,
        )
        return flat(total[0:q])

    def slab(k):
        if k > 0 and k % 2 == 0:
            return sums_buf.at[k // 2 - 1]
        return plain_buf.at[(k + 1) // 2]

    def gather_start(k, top, bottom, partials=()):
        buffer = slab(k)
        buffer[me, 0:q] = lanes(top)
        for place, partial in enumerate(partials):
            buffer[me, q + place:q + place + 1] = partial
        hsend_buf[k] = lanes(bottom)
        send_all(lambda to: buffer.at[me], buffer.at[me], gsend.at[k], grecv.at[k])
        halo_copy(k).start()

    def halo_copy(k):
        return pltpu.make_async_remote_copy(
            src_ref=hsend_buf.at[k], dst_ref=hrecv_buf.at[k], send_sem=hsend.at[k],
            recv_sem=hrecv.at[k], device_id=device(1), device_id_type=MESH,
        )

    def own_ends(top):
        own = jnp.concatenate(
            [lanes(top), jnp.zeros((pick_own.shape[0] - q, 128), jnp.float32)], axis=0
        )
        return ends(own, hot_own, pick_own)

    def gather_end(k):
        buffer = slab(k)
        wait_all(buffer, grecv.at[k])
        halo_copy(k).wait_recv()
        for j in range(n):
            faces[j * q:(j + 1) * q] = buffer[j, 0:q]
        above = jnp.where(me == 0, 0.0, flat(hrecv_buf[k]))
        below = jnp.where(me == n - 1, 0.0, flat(buffer[lax.rem(me + 1, n), 0:q]))
        return ends(faces[...], hot_other, pick_other), above, below

    def lane_sum(row):
        return jnp.sum(lanes(row), axis=0, keepdims=True)

    first_row, last_row = pl.ds(0, 1), pl.ds(rows - 1, 1)

    for copy in inputs[:6]:
        copy.wait()
    records()
    inputs[6].wait()
    pl.semaphore_wait(barrier, n - 1)
    send_all(lambda to: rsend_buf.at[to], rrecv_buf.at[me], rsend.at[0], rrecv.at[0])
    gather_start(0, start_ref[first_row], start_ref[last_row])
    rrecv_buf[me] = rsend_buf[me]
    inputs[7].wait()
    inputs[8].wait()
    kt[...] = operator(start_ref[...], shift_ref[...]) - heat_ref[...]
    wait_all(rrecv_buf, rrecv.at[0])
    live = tables()
    gap_t = own_ends(start_ref[first_row])
    gap_other, above, below = gather_end(0)
    gap_t = gap_t + gap_other
    kt[first_row] = kt[first_row] - above
    kt[last_row] = kt[last_row] - below
    top, bottom = -kt[first_row], -kt[last_row]

    for newton in range(NEWTON):
        first, second = 1 + 2 * newton, 2 + 2 * newton
        top = top - lift_of(live * (2.0 * gap_t - arctan(gap_t)))
        gather_start(first, top, bottom)
        if newton > 0:
            kt[...] = kt[...] + (step_0 * w0[...] + step_w * kw0[...])
            kt[first_row] = kt[first_row] - step_0 * lift_0
            temp_ref[...] = temp_ref[...] + (step_0 * r0[...] + step_w * w0[...])
        else:
            temp_ref[...] = start_ref[...]
        r0[...] = -kt[...]
        r0[first_row] = top
        r0[last_row] = bottom
        w0[...] = operator(r0[...], shift_ref[...])
        squares = partial_sum(r0[...] * r0[...])
        inner = partial_sum(r0[...] * w0[...])
        slope = live * (2.0 - 1.0 / (1.0 + gap_t * gap_t))
        gap_0 = own_ends(top)
        gap_other, above, below = gather_end(first)
        gap_0 = gap_0 + gap_other
        lift_0 = lift_of(slope * gap_0)
        w0[first_row] = w0[first_row] + (lift_0 - above)
        w0[last_row] = w0[last_row] - below
        inner = inner + lane_sum(top * (lift_0 - above) - bottom * below)

        gather_start(second, w0[first_row], w0[last_row], (squares, inner))
        kw0[...] = operator(w0[...], shift_ref[...])
        gap_w = own_ends(w0[first_row])
        gap_other, above, below = gather_end(second)
        gap_w = gap_w + gap_other
        lift_w = lift_of(slope * gap_w)
        totals = whole_sum(jnp.sum(slab(second)[:, q:q + 2], axis=0))
        rr, curve = totals[0:1], totals[1:2]
        alpha = rr / curve
        kw0[first_row] = kw0[first_row] - above
        kw0[last_row] = kw0[last_row] - below
        resid = r0[...] - alpha * w0[...]
        fbuf[newton, me, 0:1] = partial_sum(resid * resid)
        fbuf[newton, me, 1:2] = partial_sum(resid * w0[...])
        fbuf[newton, me, 2:3] = partial_sum(
            resid * (w0[...] - alpha * kw0[...])
        ) - alpha * lane_sum(resid[0:1] * lift_w)
        send_all(
            lambda to: fbuf.at[newton, me], fbuf.at[newton, me], fsend.at[newton], frecv.at[newton]
        )
        wait_all(fbuf.at[newton], frecv.at[newton])
        totals = whole_sum(jnp.sum(fbuf[newton, :, 0:3], axis=0))
        rr_next, cross, inner = totals[0:1], totals[1:2], totals[2:3]
        beta = rr_next / rr
        alpha_next = rr_next / (inner + 2.0 * beta * cross + beta * beta * curve)
        step_0 = alpha + alpha_next * (1.0 + beta)
        step_w = -(alpha_next * alpha)
        gap_t = gap_t + (step_0 * gap_0 + step_w * gap_w)
        top = -(
            kt[first_row] + (step_0 * (w0[first_row] - lift_0) + step_w * kw0[first_row])
        )
        bottom = -(kt[last_row] + (step_0 * w0[last_row] + step_w * kw0[last_row]))

    temp_ref[...] = temp_ref[...] + (step_0 * r0[...] + step_w * w0[...])
    outputs = [
        pltpu.make_async_copy(temp_ref, temp_out, stores.at[0]),
        pltpu.make_async_copy(final_ref, final_out, stores.at[1]),
    ]
    outputs[0].start()
    final_ref[...] = kt[...] + (step_0 * w0[...] + step_w * kw0[...])
    final_ref[first_row] = lift_of(live * (2.0 * gap_t - arctan(gap_t))) - top
    outputs[1].start()

    for k in range(GATHERS):
        wait_all(slab(k), gsend.at[k])
        halo_copy(k).wait_send()
    wait_all(rsend_buf, rsend.at[0])
    for k in range(NEWTON):
        wait_all(fbuf.at[k], fsend.at[k])
    for copy in outputs:
        copy.wait()


def settle(first_in, second_in, first_out, second_out, hold, loads, stores):
    count, height = hold.shape[0] // 2, hold.shape[1]
    moves = []
    for k in range(2 * count):
        source = (first_in, second_in)[k // count]
        target = (first_out, second_out)[k // count]
        here = pl.ds(k % count * height, height)
        moves.append((
            pltpu.make_async_copy(source.at[here], hold.at[k], loads.at[k]),
            pltpu.make_async_copy(hold.at[k], target.at[here], stores.at[k]),
        ))
    for load, _ in moves:
        load.start()
    for load, store in moves:
        load.wait()
        store.start()
    for _, store in moves:
        store.wait()


def on_device(heat, start, shift, slave, master, d_weight, m_weight, gap_cond, active):
    n = lax.axis_size("sub")
    rows, width = heat.shape
    pairs = slave.shape[0]
    q = width // 128
    slots = pairs // 8
    listed = 2 * n * slots
    tall = (q + 2 + 7) // 8 * 8
    own_rows = (q + 15) // 16 * 16
    field = pltpu.VMEM((rows, width), jnp.float32)
    whole = lambda x: pltpu.VMEM(x.shape, x.dtype)
    sems = lambda count: pltpu.SemaphoreType.DMA((count,))
    hbm = pl.BlockSpec(memory_space=pltpu.HBM)
    operands = (heat, start, shift) + tuple(
        x.reshape(1, pairs) for x in (slave, master, d_weight, m_weight, gap_cond, active)
    )
    results = pl.pallas_call(
        functools.partial(kernel, n),
        out_shape=(jax.ShapeDtypeStruct((rows, width), jnp.float32),) * 2,
        in_specs=[hbm] * 9,
        out_specs=(hbm, hbm),
        scratch_shapes=[field, field] + [whole(x) for x in operands] + [
            pltpu.VMEM((PARTS * 128, listed), jnp.bfloat16),
            pltpu.VMEM((PARTS * 128, listed), jnp.bfloat16),
            pltpu.VMEM((listed, 128), jnp.bfloat16),
            pltpu.VMEM((own_rows, listed), jnp.float32),
            pltpu.VMEM((n * q, listed), jnp.float32),
            pltpu.VMEM((n * q, 128), jnp.float32),
            field, field, field, field,
            pltpu.VMEM((1 + NEWTON, n, q, 128), jnp.float32),
            pltpu.VMEM((NEWTON, n, tall, 128), jnp.float32),
            pltpu.VMEM((GATHERS, q, 128), jnp.float32),
            pltpu.VMEM((GATHERS, q, 128), jnp.float32),
            pltpu.VMEM((n, 8, slots), jnp.float32),
            pltpu.VMEM((n, 8, slots), jnp.float32),
            pltpu.VMEM((NEWTON, n, 4, 128), jnp.float32),
            sems(9), sems(2), sems(GATHERS), sems(GATHERS), sems(GATHERS), sems(GATHERS),
            sems(1), sems(1), sems(NEWTON), sems(NEWTON),
        ],
        compiler_params=pltpu.CompilerParams(
            collective_id=0, has_side_effects=True, vmem_limit_bytes=64 * 2**20
        ),
    )(*operands)
    pieces = 4
    return pl.pallas_call(
        settle,
        out_shape=(jax.ShapeDtypeStruct((rows, width), jnp.float32),) * 2,
        in_specs=[hbm] * 2,
        out_specs=(hbm, hbm),
        scratch_shapes=[
            pltpu.VMEM((2 * pieces, rows // pieces, width), jnp.float32),
            sems(2 * pieces), sems(2 * pieces),
        ],
        compiler_params=pltpu.CompilerParams(vmem_limit_bytes=64 * 2**20),
    )(*results)


def solution(mesh):
    field = P(("groups", "sub"), None)
    pair = P(("groups", "sub"))
    return jax.shard_map(
        on_device, mesh=mesh, in_specs=(field,) * 3 + (pair,) * 6, out_specs=(field, field),
        check_vma=False,
    )
```
